512 devices in a mesh: group: 8 (over y_hi, core), node: 8 (over y_lo, x), gpu: 8 (over z).
Axes of the slice: x: 4, y: 8 (y_hi: 4, y_lo: 2; y = y_hi * 2 + y_lo), z: 8, core: 2. Of those that a mesh axis runs over, the one named last changes fastest.
Arguments:
- tokens: bfloat16 [65536, 12288], P(('group', 'node', 'gpu')), may hold values from -24 to 24
- weight: bfloat16 [12288, 256], P(('node', 'gpu')), may hold values from -0.0546875 to 0.0546875
- grad_out: bfloat16 [65536, 256], P(('group', 'node', 'gpu')), may hold values from -0.0625 to 0.0625
Outputs:
- output: bfloat16 [65536, 256], P(('group', 'node', 'gpu'))
- weight_grad: float32 [12288, 256], P(('node', 'gpu'))
The draws below stay inside these ranges and needn't reach their ends.
All inputs are finite; a program needn't handle non-finite values.
Results may differ from the reference program's by a relative error of at most 0.0029.
Values may be sent and summed in bfloat16 or wider, within the bound.
No kernel may reach another device: no remote copies, remote signals or barrier semaphores. Data moves between devices by JAX's collectives and lax.ppermute only.
A program may use at most 128 MiB of HBM per device.

```python
import jax
import jax.numpy as jnp
from jax import lax

D = 12288
COLS = 256
TOK_DEV = 128
TOKENS = 65536


def spiked(result, own_key, source, target, blocks, factor):
    def block_of(dim):
        return (jnp.arange(result.shape[dim]) // (result.shape[dim] // blocks)).reshape((-1,) + (1,) * (result.ndim - 1 - dim))

    near = jax.random.permutation(own_key, blocks)[block_of(target)]
    far = (block_of(target) + blocks // 2) % blocks
    return jnp.where((block_of(source) == near) | (block_of(source) == far), factor * result, result)


def block_levels(key, shape, shards, least, top_value):
    def one(axis_at, shards_of):
        heights = jax.random.uniform(jax.random.fold_in(jax.random.fold_in(key, 6), axis_at), (shards_of,), jnp.float32, least / len(shards), top_value / len(shards))
        return jnp.repeat(jnp.exp(heights), shape[axis_at] // shards_of).reshape((-1,) + (1,) * (len(shape) - axis_at - 1))

    loudness = one(*shards[0])
    for cut in shards[1:]:
        loudness = loudness * one(*cut)
    return loudness


def centred(stream_key, shape, width, limit, shards=(), kind=jnp.bfloat16):
    result = jax.random.normal(stream_key, shape, jnp.float32) * width
    if len(shards) > 0:
        result = block_levels(stream_key, shape, shards, -0.22, 0.18) * result
    return jnp.clip(result, min=-limit, max=limit).astype(kind)


def gaussian_with(stream_key, extent, width, bound, split, heavy, held_as=jnp.bfloat16):
    drawn = width * jax.random.normal(stream_key, extent, jnp.float32)
    if split:
        drawn = drawn * block_levels(stream_key, extent, split, -0.22, 0.18)
    return jnp.clip(spiked(drawn, jax.random.fold_in(stream_key, 3), *heavy), -bound, bound).astype(held_as)


def setup_inputs(seed: int = 0) -> dict:
    seeds = jax.random.split(jax.random.key(seed), 4)
    return {
        "tokens": gaussian_with(seeds[0], (TOKENS, D), 1.0, 24.0, ((0, 512),), (0, 1, 512, 6.0)),
        "weight": centred(seeds[1], (D, COLS), D ** -0.5, 0.0546875, ((0, 64),)),
        "grad_out": centred(seeds[2], (TOKENS, COLS), (TOKENS ** -0.5), 0.0625, ((0, 512),)),
    }


def reference(tokens, weight, grad_out):
    output = jnp.dot(tokens, weight, preferred_element_type=jnp.float32).astype(jnp.bfloat16)
    count_blocks = tokens.shape[0] // TOK_DEV
    token_blocks = tokens.reshape(count_blocks, TOK_DEV, D)
    grad_blocks = grad_out.reshape(count_blocks, TOK_DEV, COLS)

    def accumulate(running, block_pair):
        local_term = jnp.dot(block_pair[0].T, block_pair[1], preferred_element_type=jnp.float32)
        rounded = lax.optimization_barrier(local_term.astype(jnp.bfloat16))
        return running + rounded.astype(jnp.float32), None

    weight_grad, unused = lax.scan(accumulate, jnp.zeros((D, COLS), jnp.float32), (token_blocks, grad_blocks))
    return output, weight_grad
```

```python
import jax
import jax.numpy as jnp
from jax import lax
from jax.sharding import Mesh, PartitionSpec as P


def local(tokens, weight, grad_out):
    rows, width = tokens.shape
    shard, cols = weight.shape
    sharers = lax.axis_size(("c", "x"))
    lines = lax.axis_size(("yh", "yl"))
    depth = lax.axis_size("z")
    part = width // sharers
    piece = shard // lines

    blocks = jnp.stack([tokens[:, k * part : (k + 1) * part] for k in range(sharers)])
    blocks = lax.all_to_all(blocks, ("c", "x"), 0, 0)
    blocks = blocks.reshape(sharers * rows, part)

    swap = [(0, 0), (1, 2), (2, 1), (3, 3)]
    mine = lax.ppermute(weight, ("c", "yl"), swap)
    mine = lax.all_gather(mine, "z", axis=0, tiled=True)

    grads = lax.all_gather(grad_out, ("c", "x"), axis=0, tiled=True)

    term = lax.dot_general(
        blocks, grads, (((0,), (0,)), ((), ())), preferred_element_type=jnp.float32
    ).astype(jnp.bfloat16)
    term = term.reshape(depth, lines, piece, cols).transpose(1, 0, 2, 3)
    term = term.reshape(lines * depth, piece, cols)
    term = lax.all_to_all(term, ("yh", "yl", "z"), 0, 0)
    summed = jnp.sum(term, axis=0, dtype=jnp.float32)

    partial = jnp.dot(blocks, mine, preferred_element_type=jnp.float32)
    partial = lax.all_to_all(partial.reshape(sharers, rows, cols), ("c", "x"), 0, 0)
    output = jnp.sum(partial, axis=0).astype(jnp.bfloat16)

    spread = jnp.broadcast_to(summed[None], (lines, piece, cols))
    spread = lax.all_to_all(spread, ("yh", "yl"), 0, 0).reshape(shard, cols)
    other = lax.ppermute(spread, "c", [(0, 1), (1, 0)])
    own = lax.axis_index("c") == lax.axis_index("yl")
    return output, jnp.where(own, spread, other)


def solution(mesh):
    inner = Mesh(mesh.devices.reshape(4, 2, 2, 4, 8), ("yh", "c", "yl", "x", "z"))
    rows = P(("yh", "c", "yl", "x", "z"), None)
    owners = P(("yl", "x", "z"), None)
    return jax.shard_map(
        local,
        mesh=inner,
        in_specs=(rows, owners, rows),
        out_specs=(rows, owners),
        check_vma=False,
    )
```

```python
import jax
import jax.numpy as jnp
from jax import lax
from jax.experimental import pallas as pl
from jax.experimental.pallas import tpu as pltpu
from jax.sharding import Mesh, PartitionSpec as P

PARAMS = pltpu.CompilerParams(vmem_limit_bytes=32 * 1024 * 1024)


def pack(tokens, grad_out, sharers):
    rows, width = tokens.shape
    cols = grad_out.shape[1]
    part = width // sharers

    def body(t_ref, g_ref, o_ref):
        o_ref[0, :, :part] = t_ref[...]
        o_ref[0, :, part:] = g_ref[...]

    return pl.pallas_call(
        body,
        grid=(sharers,),
        in_specs=[
            pl.BlockSpec((rows, part), lambda k: (0, k)),
            pl.BlockSpec((rows, cols), lambda k: (0, 0)),
        ],
        out_specs=pl.BlockSpec((1, rows, part + cols), lambda k: (k, 0, 0)),
        out_shape=jax.ShapeDtypeStruct((sharers, rows, part + cols), tokens.dtype),
        compiler_params=PARAMS,
    )(tokens, grad_out)


def terms(packed, part, depth, yh, yl):
    sharers, rows, both = packed.shape
    cols = both - part
    shard = part // depth
    high, wide = shard // yh, cols // yl
    step = 2

    def body(t_ref, g_ref, o_ref):
        t = t_ref[...].reshape(sharers * rows, step * shard)
        g = g_ref[...].reshape(sharers * rows, cols)
        term = lax.dot_general(
            t, g, (((0,), (0,)), ((), ())), preferred_element_type=jnp.float32
        )
        for z in range(step):
            for i in range(yh):
                at = z * shard + i * high
                for j in range(yl):
                    o_ref[i, j, z] = term[
                        at : at + high, j * wide : (j + 1) * wide
                    ].astype(o_ref.dtype)

    return pl.pallas_call(
        body,
        grid=(depth // step,),
        in_specs=[
            pl.BlockSpec((sharers, rows, step * shard), lambda k: (0, 0, k)),
            pl.BlockSpec((sharers, rows, cols), lambda k: (0, 0, part // cols)),
        ],
        out_specs=pl.BlockSpec((yh, yl, step, high, wide), lambda k: (0, 0, k, 0, 0)),
        out_shape=jax.ShapeDtypeStruct((yh, yl, depth, high, wide), packed.dtype),
        compiler_params=PARAMS,
    )(packed, packed)


def project(packed, weight):
    sharers, rows, both = packed.shape
    part, cols = weight.shape

    def body(t_ref, w_ref, o_ref):
        o_ref[0] = jnp.dot(t_ref[0], w_ref[...], preferred_element_type=jnp.float32)

    return pl.pallas_call(
        body,
        grid=(sharers,),
        in_specs=[
            pl.BlockSpec((1, rows, part), lambda k: (k, 0, 0)),
            pl.BlockSpec((part, cols), lambda k: (0, 0)),
        ],
        out_specs=pl.BlockSpec((1, rows, cols), lambda k: (k, 0, 0)),
        out_shape=jax.ShapeDtypeStruct((sharers, rows, cols), jnp.float32),
        compiler_params=PARAMS,
    )(packed, weight)


def local(tokens, weight, grad_out):
    rows, width = tokens.shape
    shard, cols = weight.shape
    sharers = lax.axis_size(("c", "x"))
    yh, yl, depth = lax.axis_size("yh"), lax.axis_size("yl"), lax.axis_size("z")
    part = width // sharers

    mine = lax.ppermute(weight, ("c", "yl"), [(0, 0), (1, 2), (2, 1), (3, 3)])
    packed = pack(tokens, grad_out, sharers)
    packed = lax.all_to_all(packed, ("c", "x"), 0, 0)
    mine = jnp.broadcast_to(mine[None], (depth, shard, cols))
    mine = lax.all_to_all(mine, "z", 0, 0).reshape(part, cols)
    packed, mine = lax.optimization_barrier((packed, mine))

    term = terms(packed, part, depth, yh, yl)
    high, wide = term.shape[-2:]
    term = term.reshape(yh * yl * depth, high, wide)
    term = lax.all_to_all(term, ("yh", "yl", "z"), 0, 0)

    partial = project(packed, mine)
    partial = lax.all_to_all(partial, ("c", "x"), 0, 0)
    output = jnp.sum(partial, axis=0).astype(jnp.bfloat16)

    summed = jnp.sum(term, axis=0, dtype=jnp.float32)
    spread = jnp.broadcast_to(summed[None], (yh * yl, high, wide))
    spread = lax.all_to_all(spread, ("yh", "yl"), 0, 0)
    other = lax.ppermute(spread, "c", [(0, 1), (1, 0)])
    own = lax.axis_index("c") == lax.axis_index("yl")
    spread = jnp.where(own, spread, other).reshape(yh, yl, high, wide)
    return output, spread.transpose(0, 2, 1, 3).reshape(shard, cols)


def solution(mesh):
    inner = Mesh(mesh.devices.reshape(4, 2, 2, 4, 8), ("yh", "c", "yl", "x", "z"))
    rows = P(("yh", "c", "yl", "x", "z"), None)
    owners = P(("yl", "x", "z"), None)
    return jax.shard_map(
        local,
        mesh=inner,
        in_specs=(rows, owners, rows),
        out_specs=(rows, owners),
        check_vma=False,
    )
```

```python
import jax
import jax.numpy as jnp
from jax import lax
from jax.experimental import pallas as pl
from jax.experimental.pallas import tpu as pltpu
from jax.sharding import Mesh, PartitionSpec as P

PARAMS = pltpu.CompilerParams(vmem_limit_bytes=32 * 1024 * 1024)


def pack(tokens, grad_out, sharers):
    rows, width = tokens.shape
    cols = grad_out.shape[1]
    part = width // sharers

    def body(t_ref, g_ref, o_ref):
        o_ref[0, :, :part] = t_ref[...]
        o_ref[0, :, part:] = g_ref[...]

    return pl.pallas_call(
        body,
        grid=(sharers,),
        in_specs=[
            pl.BlockSpec((rows, part), lambda k: (0, k)),
            pl.BlockSpec((rows, cols), lambda k: (0, 0)),
        ],
        out_specs=pl.BlockSpec((1, rows, part + cols), lambda k: (k, 0, 0)),
        out_shape=jax.ShapeDtypeStruct((sharers, rows, part + cols), tokens.dtype),
        compiler_params=PARAMS,
    )(tokens, grad_out)


def terms(packed, spot, part, depth, yh):
    sharers, rows, both = packed.shape
    cols = both - part
    shard = part // depth
    high, wide = shard // yh, cols // 2
    step = 2
    first = part // wide

    def body(spot_ref, t_ref, own_ref, other_ref, keep_ref, send_ref):
        t = t_ref[...].reshape(sharers * rows, step * shard)
        g = jnp.concatenate([own_ref[...], other_ref[...]], axis=-1)
        term = lax.dot_general(
            t,
            g.reshape(sharers * rows, cols),
            (((0,), (0,)), ((), ())),
            preferred_element_type=jnp.float32,
        )
        for z in range(step):
            for i in range(yh):
                at = z * shard + i * high
                keep_ref[i, z] = term[at : at + high, :wide]
                send_ref[i, z] = term[at : at + high, wide:]

    half = jax.ShapeDtypeStruct((yh, depth, high, wide), jnp.float32)
    half_spec = pl.BlockSpec((yh, step, high, wide), lambda k, spot: (0, k, 0, 0))
    return pl.pallas_call(
        body,
        grid_spec=pltpu.PrefetchScalarGridSpec(
            num_scalar_prefetch=1,
            grid=(depth // step,),
            in_specs=[
                pl.BlockSpec(
                    (sharers, rows, step * shard), lambda k, spot: (0, 0, k)
                ),
                pl.BlockSpec(
                    (sharers, rows, wide), lambda k, spot: (0, 0, first + spot[0])
                ),
                pl.BlockSpec(
                    (sharers, rows, wide), lambda k, spot: (0, 0, first + 1 - spot[0])
                ),
            ],
            out_specs=[half_spec, half_spec],
        ),
        out_shape=[half, half],
        compiler_params=PARAMS,
    )(spot, packed, packed, packed)


def project(packed, weight, spot, away, width):
    rows = packed.shape[1]
    part, cols = weight.shape

    def source(k, spot):
        line = 1 - spot[1] if away else spot[1]
        return line * width + lax.rem(spot[2] + k, width)

    def body(spot_ref, t_ref, w_ref, o_ref):
        o_ref[0] = jnp.dot(t_ref[0], w_ref[...], preferred_element_type=jnp.float32)

    return pl.pallas_call(
        body,
        grid_spec=pltpu.PrefetchScalarGridSpec(
            num_scalar_prefetch=1,
            grid=(width,),
            in_specs=[
                pl.BlockSpec((1, rows, part), lambda k, spot: (source(k, spot), 0, 0)),
                pl.BlockSpec((part, cols), lambda k, spot: (0, 0)),
            ],
            out_specs=pl.BlockSpec((1, rows, cols), lambda k, spot: (k, 0, 0)),
        ),
        out_shape=jax.ShapeDtypeStruct((width, rows, cols), jnp.float32),
        compiler_params=PARAMS,
    )(spot, packed, weight)


def local(tokens, weight, grad_out):
    rows, model = tokens.shape
    shard, cols = weight.shape
    sharers, width = lax.axis_size(("yl", "x")), lax.axis_size("x")
    yh, depth = lax.axis_size("yh"), lax.axis_size("z")
    part = model // sharers
    spot = jnp.stack([lax.axis_index(name) for name in ("c", "yl", "x")])
    spot = spot.astype(jnp.int32)

    packed = pack(tokens, grad_out, sharers)
    packed = lax.all_to_all(packed, ("yl", "x"), 0, 0)
    mine = lax.all_gather(weight, "z", axis=0, tiled=True)
    packed, mine = lax.optimization_barrier((packed, mine))

    keep, send = terms(packed, spot, part, depth, yh)
    high, wide = keep.shape[-2:]
    term = (keep + lax.ppermute(send, "c", [(0, 1), (1, 0)])).astype(jnp.bfloat16)
    term = lax.all_to_all(term.reshape(yh * depth, high, wide), ("yh", "z"), 0, 0)
    summed = jnp.sum(term, axis=0, dtype=jnp.float32)

    away = project(packed, mine, spot, True, width)
    near = project(packed, mine, spot, False, width)
    near = near + lax.ppermute(away, "yl", [(0, 1), (1, 0)])
    output = near[0]
    for d in range(1, width):
        shift = [(i, (i + d) % width) for i in range(width)]
        output = output + lax.ppermute(near[d], "x", shift)

    spread = jnp.broadcast_to(summed[None], (yh * 2, high, wide))
    spread = lax.all_to_all(spread, ("yh", "c"), 0, 0).reshape(yh, 2, high, wide)
    spread = spread.transpose(0, 2, 1, 3).reshape(shard, cols)
    return output.astype(jnp.bfloat16), spread


def solution(mesh):
    inner = Mesh(mesh.devices.reshape(4, 2, 2, 4, 8), ("yh", "c", "yl", "x", "z"))
    rows = P(("yh", "c", "yl", "x", "z"), None)
    owners = P(("yl", "x", "z"), None)
    return jax.shard_map(
        local,
        mesh=inner,
        in_specs=(rows, owners, rows),
        out_specs=(rows, owners),
        check_vma=False,
    )
```

```python
import jax
import jax.numpy as jnp
from jax import lax
from jax.experimental import pallas as pl
from jax.experimental.pallas import tpu as pltpu
from jax.sharding import Mesh, PartitionSpec as P

PARAMS = pltpu.CompilerParams(vmem_limit_bytes=16 * 1024 * 1024)
ALONE = pltpu.CompilerParams(vmem_limit_bytes=60 * 1024 * 1024)
SWAP = [(0, 1), (1, 0)]


def pack(tokens, grad_out, sharers):
    rows, width = tokens.shape
    cols = grad_out.shape[1]
    part = width // sharers

    def body(t_ref, g_ref, o_ref):
        o_ref[0, :, :part] = t_ref[...]
        o_ref[0, :, part:] = g_ref[...]

    return pl.pallas_call(
        body,
        grid=(sharers,),
        in_specs=[
            pl.BlockSpec((rows, part), lambda k: (0, k)),
            pl.BlockSpec((rows, cols), lambda k: (0, 0)),
        ],
        out_specs=pl.BlockSpec((1, rows, part + cols), lambda k: (k, 0, 0)),
        out_shape=jax.ShapeDtypeStruct((sharers, rows, part + cols), tokens.dtype),
        compiler_params=ALONE,
    )(tokens, grad_out)


def terms(packed, spot, part, depth):
    sharers, rows, both = packed.shape
    cols = both - part
    wide = cols // 2
    step = 2 * part // depth
    first = part // wide

    def body(spot_ref, t_ref, own_ref, other_ref, keep_ref, send_ref):
        t = t_ref[...].reshape(sharers * rows, step)
        g = jnp.concatenate([own_ref[...], other_ref[...]], axis=-1)
        term = lax.dot_general(
            t,
            g.reshape(sharers * rows, cols),
            (((0,), (0,)), ((), ())),
            preferred_element_type=jnp.float32,
        )
        keep_ref[...] = term[:, :wide]
        send_ref[...] = term[:, wide:]

    half = jax.ShapeDtypeStruct((part, wide), jnp.float32)
    half_spec = pl.BlockSpec((step, wide), lambda k, spot: (k, 0))
    return pl.pallas_call(
        body,
        grid_spec=pltpu.PrefetchScalarGridSpec(
            num_scalar_prefetch=1,
            grid=(part // step,),
            in_specs=[
                pl.BlockSpec((sharers, rows, step), lambda k, spot: (0, 0, k)),
                pl.BlockSpec(
                    (sharers, rows, wide), lambda k, spot: (0, 0, first + spot[0])
                ),
                pl.BlockSpec(
                    (sharers, rows, wide), lambda k, spot: (0, 0, first + 1 - spot[0])
                ),
            ],
            out_specs=[half_spec, half_spec],
        ),
        out_shape=[half, half],
        compiler_params=PARAMS,
    )(spot, packed, packed, packed)


def project(packed, weight, spot, away, width):
    rows = packed.shape[1]
    part, cols = weight.shape

    def source(k, spot):
        line = 1 - spot[1] if away else spot[1]
        return line * width + lax.rem(spot[2] + k, width)

    def body(spot_ref, t_ref, w_ref, o_ref):
        o_ref[0] = jnp.dot(t_ref[0], w_ref[...], preferred_element_type=jnp.float32)

    return pl.pallas_call(
        body,
        grid_spec=pltpu.PrefetchScalarGridSpec(
            num_scalar_prefetch=1,
            grid=(width,),
            in_specs=[
                pl.BlockSpec((1, rows, part), lambda k, spot: (source(k, spot), 0, 0)),
                pl.BlockSpec((part, cols), lambda k, spot: (0, 0)),
            ],
            out_specs=pl.BlockSpec((1, rows, cols), lambda k, spot: (k, 0, 0)),
        ),
        out_shape=jax.ShapeDtypeStruct((width, rows, cols), jnp.float32),
        compiler_params=PARAMS,
    )(spot, packed, weight)


def local(tokens, weight, grad_out):
    rows, model = tokens.shape
    shard, cols = weight.shape
    sharers, width = lax.axis_size(("yl", "x")), lax.axis_size("x")
    yh, depth = lax.axis_size("yh"), lax.axis_size("z")
    part = model // sharers
    spot = jnp.stack([lax.axis_index(name) for name in ("c", "yl", "x")])
    spot = spot.astype(jnp.int32)

    packed = pack(tokens, grad_out, sharers)
    packed = lax.all_to_all(packed, ("yl", "x"), 0, 0)
    mine = lax.all_gather(weight, "z", axis=0, tiled=True)
    packed, mine = lax.optimization_barrier((packed, mine))

    keep, send = terms(packed, spot, part, depth)
    term = (keep + lax.ppermute(send, "c", SWAP)).astype(jnp.bfloat16)
    away = project(packed, mine, spot, True, width)
    away, _ = lax.optimization_barrier((away, term))
    away = lax.ppermute(away, "yl", SWAP)
    term = lax.all_to_all(term.reshape(depth, shard, cols // 2), "z", 0, 0)
    summed = jnp.sum(term, axis=0, dtype=jnp.float32)

    near = project(packed, mine, spot, False, width) + away
    near, _ = lax.optimization_barrier((near, summed))
    output = near[0]
    for d in range(1, width):
        shift = [(i, (i + d) % width) for i in range(width)]
        output = output + lax.ppermute(near[d], "x", shift)

    lines = jnp.broadcast_to(summed[None], (yh, shard, cols // 2))
    half = jnp.sum(lax.all_to_all(lines, "yh", 0, 0), axis=0)
    other = lax.ppermute(half, "c", SWAP)
    first = spot[0] == 0
    weight_grad = jnp.concatenate(
        [jnp.where(first, half, other), jnp.where(first, other, half)], axis=1
    )
    return output.astype(jnp.bfloat16), weight_grad


def solution(mesh):
    inner = Mesh(mesh.devices.reshape(4, 2, 2, 4, 8), ("yh", "c", "yl", "x", "z"))
    rows = P(("yh", "c", "yl", "x", "z"), None)
    owners = P(("yl", "x", "z"), None)
    return jax.shard_map(
        local,
        mesh=inner,
        in_specs=(rows, owners, rows),
        out_specs=(rows, owners),
        check_vma=False,
    )
```

```python
import jax
import jax.numpy as jnp
from jax import lax
from jax.experimental import pallas as pl
from jax.experimental.pallas import tpu as pltpu
from jax.sharding import Mesh, PartitionSpec as P

PARAMS = pltpu.CompilerParams(vmem_limit_bytes=16 * 1024 * 1024)
SWAP = [(0, 1), (1, 0)]


def pack(tokens, grad_out, spot, part):
    rows, width = tokens.shape
    cols = grad_out.shape[1]
    kind = tokens.dtype

    def body(spot_ref, t_ref, g_ref, a_ref, b0_ref, b1_ref, b2_ref, b3_ref, sems):
        copies = []
        for flip, b_ref in enumerate((b0_ref, b1_ref, b2_ref, b3_ref)):
            yl, xl = flip // 2, flip % 2
            ours = (yl * 4 + xl) * part
            theirs = ((spot_ref[1] ^ yl) * 4 + 2 + (spot_ref[2] ^ xl)) * part
            theirs = pl.multiple_of(theirs, 128)
            for source, target in (
                (t_ref.at[:, pl.ds(ours, part)], a_ref.at[flip, :, pl.ds(0, part)]),
                (g_ref, a_ref.at[flip, :, pl.ds(part, cols)]),
                (t_ref.at[:, pl.ds(theirs, part)], b_ref.at[0, :, pl.ds(0, part)]),
                (g_ref, b_ref.at[0, :, pl.ds(part, cols)]),
            ):
                copy = pltpu.make_async_copy(source, target, sems.at[len(copies)])
                copy.start()
                copies.append(copy)
        for copy in copies:
            copy.wait()

    one = jax.ShapeDtypeStruct((1, rows, part + cols), kind)
    return pl.pallas_call(
        body,
        in_specs=[
            pl.BlockSpec(memory_space=pltpu.SMEM),
            pl.BlockSpec(memory_space=pl.ANY),
            pl.BlockSpec(memory_space=pl.ANY),
        ],
        out_specs=[pl.BlockSpec(memory_space=pl.ANY)] * 5,
        out_shape=[jax.ShapeDtypeStruct((4, rows, part + cols), kind)] + [one] * 4,
        scratch_shapes=[pltpu.SemaphoreType.DMA((16,))],
        compiler_params=pltpu.CompilerParams(vmem_limit_bytes=56 * 1024 * 1024),
    )(spot, tokens, grad_out)


def terms(packed, spot, part):
    rows, both = packed[0].shape[1:]
    cols = both - part
    wide = cols // 2
    step = part // 4
    count = len(packed)

    def body(spot_ref, *refs):
        t = [r[...].reshape(-1, step) for r in refs[:count]]
        g = [r[...].reshape(-1, cols) for r in refs[count : 2 * count]]
        t = jnp.concatenate(t, axis=0) if count > 1 else t[0]
        g = jnp.concatenate(g, axis=0) if count > 1 else g[0]
        left, right = g[:, :wide], g[:, wide:]
        first = spot_ref[0] == 0
        g = jnp.concatenate(
            [jnp.where(first, left, right), jnp.where(first, right, left)], axis=1
        )
        term = lax.dot_general(
            t, g, (((0,), (0,)), ((), ())), preferred_element_type=jnp.float32
        )
        keep_ref, send_ref = refs[2 * count :]
        keep_ref[...] = term[:, :wide]
        send_ref[...] = term[:, wide:]

    half = jax.ShapeDtypeStruct((part, wide), jnp.float32)
    half_spec = pl.BlockSpec((step, wide), lambda k, spot: (k, 0))
    return pl.pallas_call(
        body,
        grid_spec=pltpu.PrefetchScalarGridSpec(
            num_scalar_prefetch=1,
            grid=(part // step,),
            in_specs=[
                pl.BlockSpec((len(p), rows, step), lambda k, spot: (0, 0, k))
                for p in packed
            ]
            + [
                pl.BlockSpec((len(p), rows, cols), lambda k, spot: (0, 0, part // cols))
                for p in packed
            ],
            out_specs=[half_spec, half_spec],
        ),
        out_shape=[half, half],
        compiler_params=PARAMS,
    )(spot, *packed, *packed)


def project(packed, weight, spot, part, at):
    rows, cols = packed[0].shape[1], weight.shape[1]
    steps = 3
    step = part // steps
    count = len(packed)

    def body(spot_ref, *refs):
        w_ref, near_ref, away_ref = refs[count:]
        if count == 1:
            own = spot_ref[1] * 2 + spot_ref[2]
            t = [refs[0][own ^ flip] for flip in range(4)]
        else:
            t = [r[0] for r in refs[:count]]
        new = jnp.dot(
            jnp.concatenate(t, axis=0), w_ref[...], preferred_element_type=jnp.float32
        ).reshape(4, rows, cols)
        k = pl.program_id(0)

        @pl.when(k == 0)
        def _():
            near_ref[...] = new[:2]
            away_ref[...] = new[2:]

        @pl.when(k > 0)
        def _():
            near_ref[...] += new[:2]
            away_ref[...] += new[2:]

    half = jax.ShapeDtypeStruct((2, rows, cols), jnp.float32)
    half_spec = pl.BlockSpec((2, rows, cols), lambda k, spot: (0, 0, 0))
    return pl.pallas_call(
        body,
        grid_spec=pltpu.PrefetchScalarGridSpec(
            num_scalar_prefetch=1,
            grid=(steps,),
            in_specs=[
                pl.BlockSpec((len(p), rows, step), lambda k, spot: (0, 0, k))
                for p in packed
            ]
            + [pl.BlockSpec((step, cols), lambda k, spot: (at * steps + k, 0))],
            out_specs=[half_spec, half_spec],
        ),
        out_shape=[half, half],
        compiler_params=PARAMS,
    )(spot, *packed, weight)


def flips(mesh_shape):
    lines, width = mesh_shape

    def partner(i, n):
        return (i + 1) % n if i % 2 else (i - 1) % n

    flip_x = [(x, partner(x, width)) for x in range(width)]
    flip_y = [(y, partner(y, lines)) for y in range(lines)]
    flip_both = [
        (y * width + x, partner(y, lines) * width + partner(x, width))
        for y in range(lines)
        for x in range(width)
    ]
    return flip_x, flip_y, flip_both


def local(tokens, weight, grad_out):
    rows, model = tokens.shape
    shard, cols = weight.shape
    depth, yh = lax.axis_size("z"), lax.axis_size("yh")
    xs, ys = ("xh", "xl"), ("yh", "yl")
    part = shard * depth
    spot = jnp.stack([lax.axis_index(name) for name in ("c", "yl", "xl")])
    spot = spot.astype(jnp.int32)
    flip_x, flip_y, flip_both = flips((lax.axis_size(ys), lax.axis_size(xs)))

    packed, b0, b1, b2, b3 = pack(tokens, grad_out, spot, part)
    packed = lax.all_to_all(packed, ("yl", "xl"), 0, 0)
    b1 = lax.ppermute(b1, xs, flip_x)
    b2 = lax.ppermute(b2, ys, flip_y)
    b3 = lax.ppermute(b3, ys + xs, flip_both)
    mine = lax.all_gather(weight, ("xh", "z"), axis=0, tiled=True)

    halves = []
    for blocks in ([packed], [b0, b1, b2, b3]):
        keep, send = terms(blocks, spot, part)
        halves.append((keep + lax.ppermute(send, "c", SWAP)).astype(jnp.bfloat16))
    term = jnp.stack(halves).reshape(2 * depth, shard, cols // 2)
    term, mine = lax.optimization_barrier((term, mine))

    near_a, away_a = project([packed], mine, spot, part, 0)
    near_b, away_b = project([b0, b1, b2, b3], mine, spot, part, 1)
    away_a, away_b, _ = lax.optimization_barrier((away_a, away_b, term))
    near_a = near_a + lax.ppermute(away_a, "yl", SWAP)
    near_b = near_b + lax.ppermute(away_b, ys, flip_y)
    output = near_a[0] + near_b[0] + lax.ppermute(near_a[1], "xl", SWAP)
    output = output + lax.ppermute(near_b[1], xs, flip_x)

    term = lax.all_to_all(term, ("xh", "z"), 0, 0)
    summed = jnp.sum(term, axis=0, dtype=jnp.float32)
    lines = jnp.broadcast_to(summed[None], (yh, shard, cols // 2))
    half = jnp.sum(lax.all_to_all(lines, "yh", 0, 0), axis=0)
    other = lax.ppermute(half, "c", SWAP)
    first = spot[0] == 0
    weight_grad = jnp.concatenate(
        [jnp.where(first, half, other), jnp.where(first, other, half)], axis=1
    )
    return output.astype(jnp.bfloat16), weight_grad


def solution(mesh):
    inner = Mesh(
        mesh.devices.reshape(4, 2, 2, 2, 2, 8), ("yh", "c", "yl", "xh", "xl", "z")
    )
    rows = P(("yh", "c", "yl", "xh", "xl", "z"), None)
    owners = P(("yl", "xh", "xl", "z"), None)
    return jax.shard_map(
        local,
        mesh=inner,
        in_specs=(rows, owners, rows),
        out_specs=(rows, owners),
        check_vma=False,
    )
```

```python
import jax
import jax.numpy as jnp
from jax import lax
from jax.experimental import pallas as pl
from jax.experimental.pallas import tpu as pltpu
from jax.sharding import Mesh, PartitionSpec as P

PARAMS = pltpu.CompilerParams(vmem_limit_bytes=24 * 1024 * 1024)
ALONE = pltpu.CompilerParams(vmem_limit_bytes=60 * 1024 * 1024)
SWAP = [(0, 1), (1, 0)]


def pack(tokens, grad_out, sharers):
    rows, width = tokens.shape
    cols = grad_out.shape[1]
    part = width // sharers

    def body(t_ref, g_ref, o_ref, stage, t_sems, g_sems, o_sems):
        loads, stores = [], []
        for k in range(sharers):
            loads.append(
                (
                    pltpu.make_async_copy(
                        t_ref.at[:, pl.ds(k * part, part)],
                        stage.at[k, :, pl.ds(0, part)],
                        t_sems.at[k],
                    ),
                    pltpu.make_async_copy(
                        g_ref, stage.at[k, :, pl.ds(part, cols)], g_sems.at[k]
                    ),
                )
            )
            stores.append(
                pltpu.make_async_copy(stage.at[k], o_ref.at[k], o_sems.at[k])
            )
        for pair in loads:
            for copy in pair:
                copy.start()
        for pair, store in zip(loads, stores):
            for copy in pair:
                copy.wait()
            store.start()
        for store in stores:
            store.wait()

    shape = (sharers, rows, part + cols)
    return pl.pallas_call(
        body,
        in_specs=[pl.BlockSpec(memory_space=pl.ANY)] * 2,
        out_specs=pl.BlockSpec(memory_space=pl.ANY),
        out_shape=jax.ShapeDtypeStruct(shape, tokens.dtype),
        scratch_shapes=[pltpu.VMEM(shape, tokens.dtype)]
        + [pltpu.SemaphoreType.DMA((sharers,))] * 3,
        compiler_params=ALONE,
    )(tokens, grad_out)


def terms(packed, spot, part):
    sharers, rows, both = packed.shape
    cols = both - part
    wide = cols // 2
    step = 2
    steps = sharers // step

    def body(spot_ref, p_ref, keep_ref, send_ref, stage, sems):
        loads = []
        for k in range(steps):
            at = pl.ds(k * step, step)
            loads.append(
                pltpu.make_async_copy(p_ref.at[at], stage.at[at], sems.at[k])
            )
            loads[-1].start()
        first = spot_ref[0] == 0
        for k in range(steps):
            loads[k].wait()
            p = stage[k * step : (k + 1) * step].reshape(step * rows, both)
            left, right = p[:, part : part + wide], p[:, part + wide :]
            g = jnp.concatenate(
                [jnp.where(first, left, right), jnp.where(first, right, left)], axis=1
            )
            term = lax.dot_general(
                p[:, :part],
                g,
                (((0,), (0,)), ((), ())),
                preferred_element_type=jnp.float32,
            )
            if k == 0:
                keep_ref[...] = term[:, :wide]
                send_ref[...] = term[:, wide:]
            else:
                keep_ref[...] += term[:, :wide]
                send_ref[...] += term[:, wide:]

    half = jax.ShapeDtypeStruct((part, wide), jnp.float32)
    return pl.pallas_call(
        body,
        in_specs=[
            pl.BlockSpec(memory_space=pltpu.SMEM),
            pl.BlockSpec(memory_space=pl.ANY),
        ],
        out_specs=[pl.BlockSpec(memory_space=pltpu.VMEM)] * 2,
        out_shape=[half, half],
        scratch_shapes=[
            pltpu.VMEM(packed.shape, packed.dtype),
            pltpu.SemaphoreType.DMA((steps,)),
        ],
        compiler_params=PARAMS,
    )(spot, packed)


def project(packed, weight, spot, away, width):
    rows = packed.shape[1]
    part, cols = weight.shape
    steps = 3
    step = part // steps

    def body(spot_ref, t_ref, w_ref, o_ref):
        t = [t_ref[lax.rem(spot_ref[2] + d, width)] for d in range(width)]
        new = jnp.dot(
            jnp.concatenate(t, axis=0), w_ref[...], preferred_element_type=jnp.float32
        ).reshape(width, rows, cols)
        k = pl.program_id(0)

        @pl.when(k == 0)
        def _():
            o_ref[...] = new

        @pl.when(k > 0)
        def _():
            o_ref[...] += new

    def line(spot):
        return 1 - spot[1] if away else spot[1]

    return pl.pallas_call(
        body,
        grid_spec=pltpu.PrefetchScalarGridSpec(
            num_scalar_prefetch=1,
            grid=(steps,),
            in_specs=[
                pl.BlockSpec(
                    (width, rows, step),
                    lambda k, spot: (line(spot), 0, k),
                ),
                pl.BlockSpec((step, cols), lambda k, spot: (k, 0)),
            ],
            out_specs=pl.BlockSpec((width, rows, cols), lambda k, spot: (0, 0, 0)),
        ),
        out_shape=jax.ShapeDtypeStruct((width, rows, cols), jnp.float32),
        compiler_params=PARAMS,
    )(spot, packed, weight)


def local(tokens, weight, grad_out):
    rows, model = tokens.shape
    shard, cols = weight.shape
    sharers, width = lax.axis_size(("yl", "x")), lax.axis_size("x")
    yh, depth = lax.axis_size("yh"), lax.axis_size("z")
    part = model // sharers
    spot = jnp.stack([lax.axis_index(name) for name in ("c", "yl", "x")])
    spot = spot.astype(jnp.int32)

    packed = pack(tokens, grad_out, sharers)
    packed = lax.all_to_all(packed, ("yl", "x"), 0, 0)
    mine = lax.all_gather(weight, "z", axis=0, tiled=True)
    packed, mine = lax.optimization_barrier((packed, mine))

    keep, send = terms(packed, spot, part)
    term = (keep + lax.ppermute(send, "c", SWAP)).astype(jnp.bfloat16)
    away = project(packed, mine, spot, True, width)
    away, _ = lax.optimization_barrier((away, term))
    away = lax.ppermute(away, "yl", SWAP)
    term = lax.all_to_all(term.reshape(depth, shard, cols // 2), "z", 0, 0)
    summed = jnp.sum(term, axis=0, dtype=jnp.float32)

    near = project(packed, mine, spot, False, width)
    near, summed = lax.optimization_barrier((near, summed))
    near = near + away
    output = near[0]
    for d in range(1, width):
        shift = [(i, (i + d) % width) for i in range(width)]
        output = output + lax.ppermute(near[d], "x", shift)

    lines = jnp.broadcast_to(summed[None], (yh, shard, cols // 2))
    half = jnp.sum(lax.all_to_all(lines, "yh", 0, 0), axis=0)
    other = lax.ppermute(half, "c", SWAP)
    first = spot[0] == 0
    weight_grad = jnp.concatenate(
        [jnp.where(first, half, other), jnp.where(first, other, half)], axis=1
    )
    return output.astype(jnp.bfloat16), weight_grad


def solution(mesh):
    inner = Mesh(mesh.devices.reshape(4, 2, 2, 4, 8), ("yh", "c", "yl", "x", "z"))
    rows = P(("yh", "c", "yl", "x", "z"), None)
    owners = P(("yl", "x", "z"), None)
    return jax.shard_map(
        local,
        mesh=inner,
        in_specs=(rows, owners, rows),
        out_specs=(rows, owners),
        check_vma=False,
    )
```

```python
import jax
import jax.numpy as jnp
from jax import lax
from jax.experimental import pallas as pl
from jax.experimental.pallas import tpu as pltpu
from jax.sharding import Mesh, PartitionSpec as P

PARAMS = pltpu.CompilerParams(vmem_limit_bytes=24 * 1024 * 1024)
ALONE = pltpu.CompilerParams(vmem_limit_bytes=60 * 1024 * 1024)
SWAP = [(0, 1), (1, 0)]
CHIP = ("yh", "c", "yl", "xh", "xl")


def pack(tokens, grad_out, spot, shard):
    rows, width = tokens.shape
    cols = grad_out.shape[1]
    quads = 4
    node = width // 8
    part = width // 8
    half = shard // 2

    def body(spot_ref, t_ref, g_ref, keep_ref, send_ref, held, stage, t_sems, g_sems, o_sems):
        loads, sides = [], []
        for k in range(8):
            at = pl.ds(k * node, node)
            copy = pltpu.make_async_copy(t_ref.at[:, at], held.at[:, at], t_sems.at[k])
            copy.start()
            loads.append(copy)
        for side in range(2):
            for quad in range(quads):
                copy = pltpu.make_async_copy(
                    g_ref,
                    stage.at[side, quad, :, pl.ds(part, cols)],
                    g_sems.at[side, quad],
                )
                copy.start()
                sides.append(copy)
        for copy in sides:
            copy.wait()
        stores = []
        for quad in range(quads):
            for xh in range(2):
                k = (quad // 2) * 4 + xh * 2 + quad % 2
                loads[k].wait()
                t = held[:, k * node : (k + 1) * node]
                for side in range(2):
                    pieces = [
                        t[:, at + side * half : at + side * half + half]
                        for at in range(0, node, shard)
                    ]
                    stage[side, quad, :, xh * node // 2 : (xh + 1) * node // 2] = (
                        jnp.concatenate(pieces, axis=1)
                    )
            for n, ref in enumerate((keep_ref, send_ref)):
                copy = pltpu.make_async_copy(
                    stage.at[spot_ref[0] ^ n, quad], ref.at[quad], o_sems.at[n, quad]
                )
                copy.start()
                stores.append(copy)
        for copy in stores:
            copy.wait()

    shape = (quads, rows, part + cols)
    out = jax.ShapeDtypeStruct(shape, tokens.dtype)
    return pl.pallas_call(
        body,
        in_specs=[pl.BlockSpec(memory_space=pltpu.SMEM)]
        + [pl.BlockSpec(memory_space=pl.ANY)] * 2,
        out_specs=[pl.BlockSpec(memory_space=pl.ANY)] * 2,
        out_shape=[out, out],
        scratch_shapes=[
            pltpu.VMEM(tokens.shape, tokens.dtype),
            pltpu.VMEM((2,) + shape, tokens.dtype),
            pltpu.SemaphoreType.DMA((8,)),
            pltpu.SemaphoreType.DMA((2, quads)),
            pltpu.SemaphoreType.DMA((2, quads)),
        ],
        compiler_params=ALONE,
    )(spot, tokens, grad_out)


def terms(packed, part):
    quads, cores, rows, both = packed.shape
    cols = both - part

    def body(p_ref, o_ref, stage, total, sems):
        loads = []
        for k in range(quads):
            loads.append(
                pltpu.make_async_copy(p_ref.at[k], stage.at[k], sems.at[k])
            )
            loads[-1].start()
        for k in range(quads):
            loads[k].wait()
            p = stage[k].reshape(cores * rows, both)
            term = lax.dot_general(
                p[:, :part],
                p[:, part:],
                (((0,), (0,)), ((), ())),
                preferred_element_type=jnp.float32,
            )
            if k == 0:
                total[...] = term
            elif k < quads - 1:
                total[...] += term
            else:
                o_ref[...] = (total[...] + term).astype(o_ref.dtype)

    return pl.pallas_call(
        body,
        in_specs=[pl.BlockSpec(memory_space=pl.ANY)],
        out_specs=pl.BlockSpec(memory_space=pltpu.VMEM),
        out_shape=jax.ShapeDtypeStruct((part, cols), packed.dtype),
        scratch_shapes=[
            pltpu.VMEM(packed.shape, packed.dtype),
            pltpu.VMEM((part, cols), jnp.float32),
            pltpu.SemaphoreType.DMA((quads,)),
        ],
        compiler_params=PARAMS,
    )(packed)


def project(packed, weight, spot):
    quads, cores, rows, _ = packed.shape
    part, cols = weight.shape
    steps = 3
    step = part // steps

    def body(spot_ref, t_ref, w_ref, near_ref, away_ref):
        own = spot_ref[1] * 2 + spot_ref[2]
        t = [t_ref[own ^ flip].reshape(cores * rows, step) for flip in range(quads)]
        new = jnp.dot(
            jnp.concatenate(t, axis=0), w_ref[...], preferred_element_type=jnp.float32
        ).reshape(quads, cores, rows, cols)
        k = pl.program_id(0)

        @pl.when(k == 0)
        def _():
            near_ref[...] = new[:2]
            away_ref[...] = new[2:]

        @pl.when(k > 0)
        def _():
            near_ref[...] += new[:2]
            away_ref[...] += new[2:]

    shape = (2, cores, rows, cols)
    half = jax.ShapeDtypeStruct(shape, jnp.float32)
    half_spec = pl.BlockSpec(shape, lambda k, spot: (0, 0, 0, 0))
    return pl.pallas_call(
        body,
        grid_spec=pltpu.PrefetchScalarGridSpec(
            num_scalar_prefetch=1,
            grid=(steps,),
            in_specs=[
                pl.BlockSpec((quads, cores, rows, step), lambda k, spot: (0, 0, 0, k)),
                pl.BlockSpec((step, cols), lambda k, spot: (k, 0)),
            ],
            out_specs=[half_spec, half_spec],
        ),
        out_shape=[half, half],
        compiler_params=PARAMS,
    )(spot, packed, weight)


def partners(sizes):
    yh, cores, yl, xh, xl = sizes
    lines, width = yh * yl, xh * xl

    def place(y, c, x):
        return ((((y // yl) * cores + c) * yl + y % yl) * xh + x // xl) * xl + x % xl

    def other(i, n, c):
        if c == 0:
            return i ^ 1
        return (i + 1) % n if i % 2 else (i - 1) % n

    flip_x, flip_y, squares = [], [], []
    for y in range(lines):
        for c in range(cores):
            for x in range(width):
                flip_x.append((place(y, c, x), place(y, c, other(x, width, c))))
                flip_y.append((place(y, c, x), place(other(y, lines, c), c, x)))
                if y % 2 == 0 and x % 2 == 0:
                    ys, xs = (y, other(y, lines, c)), (x, other(x, width, c))
                    squares.append([place(a, c, b) for a in ys for b in xs])
    return squares, flip_x, flip_y


def local(tokens, weight, grad_out):
    rows, _ = tokens.shape
    shard, cols = weight.shape
    half = shard // 2
    squares, flip_x, flip_y = partners([lax.axis_size(name) for name in CHIP])
    spot = jnp.stack([lax.axis_index(name) for name in ("c", "yl", "xl")])
    spot = spot.astype(jnp.int32)

    keep, send = pack(tokens, grad_out, spot, shard)
    packed = jnp.stack([keep, lax.ppermute(send, "c", SWAP)], axis=1)
    packed = lax.all_to_all(packed, CHIP, 0, 0, axis_index_groups=squares)
    mine = lax.dynamic_slice(weight, (spot[0] * half, 0), (half, cols))
    mine = lax.all_gather(mine, ("xh", "z"), axis=0, tiled=True)
    part = mine.shape[0]
    packed, mine = lax.optimization_barrier((packed, mine))

    term = terms(packed, part).reshape(part // half, half, cols)
    near, away = project(packed, mine, spot)
    away = lax.ppermute(away, CHIP, flip_y)
    term = lax.all_to_all(term, ("xh", "z"), 0, 0)
    summed = jnp.sum(term, axis=0, dtype=jnp.float32)
    near = near + away
    near = near[0] + lax.ppermute(near[1], CHIP, flip_x)
    output = near[0] + lax.ppermute(near[1], "c", SWAP)

    lines = jnp.broadcast_to(summed[None], (lax.axis_size("yh"), half, cols))
    mid = jnp.sum(lax.all_to_all(lines, "yh", 0, 0), axis=0)
    other = lax.ppermute(mid, "c", SWAP)
    first = spot[0] == 0
    weight_grad = jnp.concatenate(
        [jnp.where(first, mid, other), jnp.where(first, other, mid)], axis=0
    )
    return output.astype(jnp.bfloat16), weight_grad


def solution(mesh):
    inner = Mesh(
        mesh.devices.reshape(4, 2, 2, 2, 2, 8), ("yh", "c", "yl", "xh", "xl", "z")
    )
    rows = P(("yh", "c", "yl", "xh", "xl", "z"), None)
    owners = P(("yl", "xh", "xl", "z"), None)
    return jax.shard_map(
        local,
        mesh=inner,
        in_specs=(rows, owners, rows),
        out_specs=(rows, owners),
        check_vma=False,
    )
```

```python
import jax
import jax.numpy as jnp
from jax import lax
from jax.experimental import pallas as pl
from jax.experimental.pallas import tpu as pltpu
from jax.sharding import Mesh, PartitionSpec as P

PARAMS = pltpu.CompilerParams(vmem_limit_bytes=24 * 1024 * 1024)
ALONE = pltpu.CompilerParams(vmem_limit_bytes=60 * 1024 * 1024)
SWAP = [(0, 1), (1, 0)]
CHIP = ("yh", "c", "yl", "xh", "xl")


def pack(tokens, grad_out, spot, shard, away, after=()):
    rows, width = tokens.shape
    cols = grad_out.shape[1]
    quads = 4
    node = width // 8
    part = width // 8
    half = shard // 2

    def body(spot_ref, t_ref, g_ref, *refs):
        o_ref, held, stage, t_sems, g_sems, o_sems = refs[len(after) :]
        loads, sides = [], []
        order = [(quad, xh) for quad in range(quads) for xh in range(2)]
        for n, (quad, xh) in enumerate(order):
            at = pl.ds(((quad // 2) * 4 + xh * 2 + quad % 2) * node, node)
            copy = pltpu.make_async_copy(t_ref.at[:, at], held.at[n], t_sems.at[n])
            copy.start()
            loads.append(copy)
        for quad in range(quads):
            copy = pltpu.make_async_copy(
                g_ref, stage.at[quad, :, pl.ds(part, cols)], g_sems.at[quad]
            )
            copy.start()
            sides.append(copy)
        family = spot_ref[0] ^ 1 if away else spot_ref[0]

        def squeeze(quad, side):
            for xh in range(2):
                t = held[quad * 2 + xh]
                pieces = [
                    t[:, at + side * half : at + side * half + half]
                    for at in range(0, node, shard)
                ]
                stage[quad, :, xh * node // 2 : (xh + 1) * node // 2] = (
                    jnp.concatenate(pieces, axis=1)
                )

        stores = []
        for quad in range(quads):
            loads[2 * quad].wait()
            loads[2 * quad + 1].wait()
            sides[quad].wait()
            for side in range(2):
                pl.when(family == side)(lambda quad=quad, side=side: squeeze(quad, side))
            target = o_ref.at[quad] if away else o_ref.at[quad, 0]
            copy = pltpu.make_async_copy(stage.at[quad], target, o_sems.at[quad])
            copy.start()
            stores.append(copy)
        for copy in stores:
            copy.wait()

    shape = (quads, rows, part + cols)
    whole = shape if away else (quads, 2, rows, part + cols)
    return pl.pallas_call(
        body,
        in_specs=[pl.BlockSpec(memory_space=pltpu.SMEM)]
        + [pl.BlockSpec(memory_space=pl.ANY)] * (2 + len(after)),
        out_specs=pl.BlockSpec(memory_space=pl.ANY),
        out_shape=jax.ShapeDtypeStruct(whole, tokens.dtype),
        scratch_shapes=[
            pltpu.VMEM((8, rows, node), tokens.dtype),
            pltpu.VMEM(shape, tokens.dtype),
            pltpu.SemaphoreType.DMA((8,)),
            pltpu.SemaphoreType.DMA((quads,)),
            pltpu.SemaphoreType.DMA((quads,)),
        ],
        compiler_params=ALONE,
    )(spot, tokens, grad_out, *after)


def insert(packed, received, after):
    quads = packed.shape[0]

    def body(p_ref, r_ref, after_ref, o_ref, sems):
        copies = [
            pltpu.make_async_copy(r_ref.at[q], o_ref.at[q, 1], sems.at[q])
            for q in range(quads)
        ]
        for copy in copies:
            copy.start()
        for copy in copies:
            copy.wait()

    return pl.pallas_call(
        body,
        in_specs=[
            pl.BlockSpec(memory_space=pltpu.HBM),
            pl.BlockSpec(memory_space=pltpu.VMEM),
            pl.BlockSpec(memory_space=pl.ANY),
        ],
        out_specs=pl.BlockSpec(memory_space=pltpu.HBM),
        out_shape=jax.ShapeDtypeStruct(packed.shape, packed.dtype),
        scratch_shapes=[pltpu.SemaphoreType.DMA((quads,))],
        input_output_aliases={0: 0},
        compiler_params=pltpu.CompilerParams(vmem_limit_bytes=57 * 1024 * 1024),
    )(packed, received, after)


def terms(packed, part):
    quads, cores, rows, both = packed.shape
    cols = both - part

    def body(p_ref, o_ref, stage, total, sems):
        loads = []
        for k in range(quads):
            loads.append(
                pltpu.make_async_copy(p_ref.at[k], stage.at[k], sems.at[k])
            )
            loads[-1].start()
        for k in range(quads):
            loads[k].wait()
            p = stage[k].reshape(cores * rows, both)
            term = lax.dot_general(
                p[:, :part],
                p[:, part:],
                (((0,), (0,)), ((), ())),
                preferred_element_type=jnp.float32,
            )
            if k == 0:
                total[...] = term
            elif k < quads - 1:
                total[...] += term
            else:
                o_ref[...] = (total[...] + term).astype(o_ref.dtype)

    return pl.pallas_call(
        body,
        in_specs=[pl.BlockSpec(memory_space=pl.ANY)],
        out_specs=pl.BlockSpec(memory_space=pltpu.VMEM),
        out_shape=jax.ShapeDtypeStruct((part, cols), packed.dtype),
        scratch_shapes=[
            pltpu.VMEM(packed.shape, packed.dtype),
            pltpu.VMEM((part, cols), jnp.float32),
            pltpu.SemaphoreType.DMA((quads,)),
        ],
        compiler_params=PARAMS,
    )(packed)


def project(packed, weight, spot):
    quads, cores, rows, _ = packed.shape
    depth, steps, _, half, cols = weight.shape
    step = depth * half

    def body(spot_ref, t_ref, w_ref, near_ref, away_ref):
        own = spot_ref[1] * 2 + spot_ref[2]
        t = [t_ref[own ^ flip].reshape(cores * rows, step) for flip in range(quads)]
        new = jnp.dot(
            jnp.concatenate(t, axis=0),
            w_ref[...].reshape(step, cols),
            preferred_element_type=jnp.float32,
        ).reshape(quads, cores, rows, cols)
        k = pl.program_id(0)

        @pl.when(k == 0)
        def _():
            near_ref[...] = new[:2]
            away_ref[...] = new[2:]

        @pl.when(k > 0)
        def _():
            near_ref[...] += new[:2]
            away_ref[...] += new[2:]

    shape = (2, cores, rows, cols)
    out = jax.ShapeDtypeStruct(shape, jnp.float32)
    out_spec = pl.BlockSpec(shape, lambda k, spot: (0, 0, 0, 0))
    return pl.pallas_call(
        body,
        grid_spec=pltpu.PrefetchScalarGridSpec(
            num_scalar_prefetch=1,
            grid=(steps,),
            in_specs=[
                pl.BlockSpec((quads, cores, rows, step), lambda k, spot: (0, 0, 0, k)),
                pl.BlockSpec(
                    (depth, 1, 1, half, cols),
                    lambda k, spot: (0, k ^ spot[3], spot[0], 0, 0),
                ),
            ],
            out_specs=[out_spec, out_spec],
        ),
        out_shape=[out, out],
        compiler_params=PARAMS,
    )(spot, packed, weight)


def partners(sizes):
    yh, cores, yl, xh, xl = sizes
    lines, width = yh * yl, xh * xl

    def place(y, c, x):
        return ((((y // yl) * cores + c) * yl + y % yl) * xh + x // xl) * xl + x % xl

    def other(i, n, c):
        if c == 0:
            return i ^ 1
        return (i + 1) % n if i % 2 else (i - 1) % n

    flip_x, flip_y, squares = [], [], []
    for y in range(lines):
        for c in range(cores):
            for x in range(width):
                flip_x.append((place(y, c, x), place(y, c, other(x, width, c))))
                flip_y.append((place(y, c, x), place(other(y, lines, c), c, x)))
                if y % 2 == 0 and x % 2 == 0:
                    ys, xs = (y, other(y, lines, c)), (x, other(x, width, c))
                    squares.append([place(a, c, b) for a in ys for b in xs])
    return squares, flip_x, flip_y


def local(tokens, weight, grad_out):
    rows, _ = tokens.shape
    shard, cols = weight.shape
    half = shard // 2
    squares, flip_x, flip_y = partners([lax.axis_size(name) for name in CHIP])
    spot = jnp.stack([lax.axis_index(name) for name in ("c", "yl", "xl", "xh")])
    spot = spot.astype(jnp.int32)

    mine = jnp.stack([weight, lax.ppermute(weight, "xh", SWAP)])
    send = pack(tokens, grad_out, spot, shard, True)
    packed = pack(tokens, grad_out, spot, shard, False, (send,))
    packed = insert(packed, lax.ppermute(send, "c", SWAP), mine)
    packed = lax.all_to_all(packed, CHIP, 0, 0, axis_index_groups=squares)
    part = packed.shape[-1] - cols

    mine = lax.all_gather(mine, "z", axis=0)
    mine = mine.reshape(mine.shape[:2] + (2, half, cols))

    term = terms(packed, part).reshape(part // half, half, cols)
    term, mine = lax.optimization_barrier((term, mine))
    near, away = project(packed, mine, spot)
    away = lax.ppermute(away, CHIP, flip_y)
    term = lax.all_to_all(term, ("xh", "z"), 0, 0)
    summed = jnp.sum(term, axis=0, dtype=jnp.float32)
    near, _ = lax.optimization_barrier((near, summed))
    near = near + away
    near = near[0] + lax.ppermute(near[1], CHIP, flip_x)

    lines = jnp.broadcast_to(summed[None], (lax.axis_size("yh"), half, cols))
    mid = jnp.sum(lax.all_to_all(lines, "yh", 0, 0), axis=0)
    other = lax.ppermute(mid, "c", SWAP)
    near, _ = lax.optimization_barrier((near, mid))
    output = near[0] + lax.ppermute(near[1], "c", SWAP)
    first = spot[0] == 0
    weight_grad = jnp.concatenate(
        [jnp.where(first, mid, other), jnp.where(first, other, mid)], axis=0
    )
    return output.astype(jnp.bfloat16), weight_grad


def solution(mesh):
    inner = Mesh(
        mesh.devices.reshape(4, 2, 2, 2, 2, 8), ("yh", "c", "yl", "xh", "xl", "z")
    )
    rows = P(("yh", "c", "yl", "xh", "xl", "z"), None)
    owners = P(("yl", "xh", "xl", "z"), None)
    return jax.shard_map(
        local,
        mesh=inner,
        in_specs=(rows, owners, rows),
        out_specs=(rows, owners),
        check_vma=False,
    )
```

```python
import jax
import jax.numpy as jnp
from jax import lax
from jax.experimental import pallas as pl
from jax.experimental.pallas import tpu as pltpu
from jax.sharding import Mesh, PartitionSpec as P

PARAMS = pltpu.CompilerParams(vmem_limit_bytes=32 * 1024 * 1024)
ALONE = pltpu.CompilerParams(vmem_limit_bytes=60 * 1024 * 1024)
SWAP = [(0, 1), (1, 0)]
CHIP = ("yh", "c", "yl", "xh", "xl")


def pack(tokens, grad_out):
    rows, width = tokens.shape
    cols = grad_out.shape[1]
    quads, node = 4, width // 8

    def body(t_ref, g_ref, o_ref, stage, t_sems, g_sems, o_sems):
        loads, stores = [], []
        for quad in range(quads):
            group = []
            for xh in range(2):
                at = ((quad // 2) * 4 + xh * 2 + quad % 2) * node
                group.append(
                    pltpu.make_async_copy(
                        t_ref.at[:, pl.ds(at, node)],
                        stage.at[quad, :, pl.ds(xh * node, node)],
                        t_sems.at[quad, xh],
                    )
                )
            group.append(
                pltpu.make_async_copy(
                    g_ref, stage.at[quad, :, pl.ds(2 * node, cols)], g_sems.at[quad]
                )
            )
            loads.append(group)
            stores.append(
                pltpu.make_async_copy(stage.at[quad], o_ref.at[quad], o_sems.at[quad])
            )
        for group in loads:
            for copy in group:
                copy.start()
        for group, store in zip(loads, stores):
            for copy in group:
                copy.wait()
            store.start()
        for store in stores:
            store.wait()

    shape = (quads, rows, 2 * node + cols)
    return pl.pallas_call(
        body,
        in_specs=[pl.BlockSpec(memory_space=pl.ANY)] * 2,
        out_specs=pl.BlockSpec(memory_space=pl.ANY),
        out_shape=jax.ShapeDtypeStruct(shape, tokens.dtype),
        scratch_shapes=[
            pltpu.VMEM(shape, tokens.dtype),
            pltpu.SemaphoreType.DMA((quads, 2)),
            pltpu.SemaphoreType.DMA((quads,)),
            pltpu.SemaphoreType.DMA((quads,)),
        ],
        compiler_params=ALONE,
    )(tokens, grad_out)


def terms(packed, spot, part):
    sharers, rows, both = packed.shape
    cols = both - part
    wide = cols // 2
    step = 2
    steps = sharers // step

    def body(spot_ref, p_ref, keep_ref, send_ref, stage, sems):
        loads = []
        for k in range(steps):
            at = pl.ds(k * step, step)
            loads.append(
                pltpu.make_async_copy(p_ref.at[at], stage.at[at], sems.at[k])
            )
            loads[-1].start()
        first = spot_ref[0] == 0
        for k in range(steps):
            loads[k].wait()
            p = stage[k * step : (k + 1) * step].reshape(step * rows, both)
            left, right = p[:, part : part + wide], p[:, part + wide :]
            g = jnp.concatenate(
                [jnp.where(first, left, right), jnp.where(first, right, left)], axis=1
            )
            term = lax.dot_general(
                p[:, :part],
                g,
                (((0,), (0,)), ((), ())),
                preferred_element_type=jnp.float32,
            )
            if k == 0:
                keep_ref[...] = term[:, :wide]
                send_ref[...] = term[:, wide:]
            else:
                keep_ref[...] += term[:, :wide]
                send_ref[...] += term[:, wide:]

    half = jax.ShapeDtypeStruct((part, wide), jnp.float32)
    return pl.pallas_call(
        body,
        in_specs=[
            pl.BlockSpec(memory_space=pltpu.SMEM),
            pl.BlockSpec(memory_space=pl.ANY),
        ],
        out_specs=[pl.BlockSpec(memory_space=pltpu.VMEM)] * 2,
        out_shape=[half, half],
        scratch_shapes=[
            pltpu.VMEM(packed.shape, packed.dtype),
            pltpu.SemaphoreType.DMA((steps,)),
        ],
        compiler_params=PARAMS,
    )(spot, packed)


def project(packed, mine, other, spot):
    quads, rows, both = packed.shape
    depth, xhs, shard, wide = mine.shape
    part, cols = depth * xhs * shard, 2 * wide

    def body(spot_ref, p_ref, m_ref, r_ref, near_ref, away_ref, stage, whole, sems):
        core, yl, xl, xh, z = (spot_ref[i] for i in range(5))
        loads = []
        for flip in range(quads):
            loads.append(
                pltpu.make_async_copy(
                    p_ref.at[(yl * 2 + xl) ^ flip], stage.at[flip], sems.at[flip]
                )
            )
            loads[-1].start()
        for back in range(depth):
            at_z = lax.rem(z + depth - back, depth)
            for slot in range(xhs):
                left = jnp.where(core == 0, m_ref[back, slot], r_ref[back, slot])
                right = jnp.where(core == 0, r_ref[back, slot], m_ref[back, slot])
                whole[xh ^ slot, at_z] = jnp.concatenate([left, right], axis=1)
        for load in loads:
            load.wait()
        t = stage[...].reshape(quads * rows, both)[:, :part]
        new = jnp.dot(
            t, whole[...].reshape(part, cols), preferred_element_type=jnp.float32
        ).reshape(quads, rows, cols)
        near_ref[...] = new[:2]
        away_ref[...] = new[2:]

    out = jax.ShapeDtypeStruct((2, rows, cols), jnp.float32)
    return pl.pallas_call(
        body,
        in_specs=[
            pl.BlockSpec(memory_space=pltpu.SMEM),
            pl.BlockSpec(memory_space=pl.ANY),
            pl.BlockSpec(memory_space=pltpu.VMEM),
            pl.BlockSpec(memory_space=pltpu.VMEM),
        ],
        out_specs=[pl.BlockSpec(memory_space=pltpu.VMEM)] * 2,
        out_shape=[out, out],
        scratch_shapes=[
            pltpu.VMEM(packed.shape, packed.dtype),
            pltpu.VMEM((xhs, depth, shard, cols), mine.dtype),
            pltpu.SemaphoreType.DMA((quads,)),
        ],
        compiler_params=PARAMS,
    )(spot, packed, mine, other)


def partners(sizes):
    yh, cores, yl, xh, xl = sizes
    lines, width = yh * yl, xh * xl

    def place(y, c, x):
        return ((((y // yl) * cores + c) * yl + y % yl) * xh + x // xl) * xl + x % xl

    def other(i, n, c):
        if c == 0:
            return i ^ 1
        return (i + 1) % n if i % 2 else (i - 1) % n

    flip_x, flip_y, squares = [], [], []
    for y in range(lines):
        for c in range(cores):
            for x in range(width):
                flip_x.append((place(y, c, x), place(y, c, other(x, width, c))))
                flip_y.append((place(y, c, x), place(other(y, lines, c), c, x)))
                if y % 2 == 0 and x % 2 == 0:
                    ys, xs = (y, other(y, lines, c)), (x, other(x, width, c))
                    squares.append([place(a, c, b) for a in ys for b in xs])
    return squares, flip_x, flip_y


def local(tokens, weight, grad_out):
    shard, cols = weight.shape
    wide = cols // 2
    depth = lax.axis_size("z")
    squares, flip_x, flip_y = partners([lax.axis_size(name) for name in CHIP])
    spot = jnp.stack([lax.axis_index(name) for name in ("c", "yl", "xl", "xh", "z")])
    spot = spot.astype(jnp.int32)

    mine = jnp.where(spot[0] == 0, weight[:, :wide], weight[:, wide:])
    mine = jnp.stack([mine, lax.ppermute(mine, "xh", SWAP)])
    packed = pack(tokens, grad_out)
    packed = lax.all_to_all(packed, CHIP, 0, 0, axis_index_groups=squares)
    part = packed.shape[-1] - cols
    gathered = [mine]
    for back in range(1, depth):
        shift = [(i, (i + back) % depth) for i in range(depth)]
        gathered.append(lax.ppermute(mine, "z", shift))
    packed, *gathered = lax.optimization_barrier((packed, *gathered))

    keep, send = terms(packed, spot, part)
    term = (keep + lax.ppermute(send, "c", SWAP)).astype(jnp.bfloat16)
    mine = jnp.stack(gathered)
    mine, _ = lax.optimization_barrier((mine, send))
    other = lax.ppermute(mine, "c", SWAP)
    term = lax.all_to_all(term.reshape(-1, shard, wide), ("xh", "z"), 0, 0)
    summed = jnp.sum(term, axis=0, dtype=jnp.float32)

    near, away = project(packed, mine, other, spot)
    away = lax.ppermute(away, CHIP, flip_y)
    near, _ = lax.optimization_barrier((near, summed))
    near = near + away
    output = near[0] + lax.ppermute(near[1], CHIP, flip_x)

    lines = jnp.broadcast_to(summed[None], (lax.axis_size("yh"), shard, wide))
    half = jnp.sum(lax.all_to_all(lines, "yh", 0, 0), axis=0)
    other = lax.ppermute(half, "c", SWAP)
    first = spot[0] == 0
    weight_grad = jnp.concatenate(
        [jnp.where(first, half, other), jnp.where(first, other, half)], axis=1
    )
    return output.astype(jnp.bfloat16), weight_grad


def solution(mesh):
    inner = Mesh(
        mesh.devices.reshape(4, 2, 2, 2, 2, 8), ("yh", "c", "yl", "xh", "xl", "z")
    )
    rows = P(("yh", "c", "yl", "xh", "xl", "z"), None)
    owners = P(("yl", "xh", "xl", "z"), None)
    return jax.shard_map(
        local,
        mesh=inner,
        in_specs=(rows, owners, rows),
        out_specs=(rows, owners),
        check_vma=False,
    )
```

```python
import jax
import jax.numpy as jnp
from jax import lax
from jax.experimental import pallas as pl
from jax.experimental.pallas import tpu as pltpu
from jax.sharding import Mesh, PartitionSpec as P

PARAMS = pltpu.CompilerParams(vmem_limit_bytes=32 * 1024 * 1024)
ALONE = pltpu.CompilerParams(vmem_limit_bytes=60 * 1024 * 1024)
SWAP = [(0, 1), (1, 0)]
CHIP = ("yh", "c", "yl", "xh", "xl")


def pack(tokens, grad_out):
    rows, width = tokens.shape
    cols = grad_out.shape[1]
    quads, node = 4, width // 8

    def body(t_ref, g_ref, o_ref, stage, t_sems, g_sems, o_sems):
        loads, stores = [], []
        for quad in range(quads):
            group = []
            for xh in range(2):
                at = ((quad // 2) * 4 + xh * 2 + quad % 2) * node
                group.append(
                    pltpu.make_async_copy(
                        t_ref.at[:, pl.ds(at, node)],
                        stage.at[quad, :, pl.ds(xh * node, node)],
                        t_sems.at[quad, xh],
                    )
                )
            group.append(
                pltpu.make_async_copy(
                    g_ref, stage.at[quad, :, pl.ds(2 * node, cols)], g_sems.at[quad]
                )
            )
            loads.append(group)
            stores.append(
                pltpu.make_async_copy(stage.at[quad], o_ref.at[quad], o_sems.at[quad])
            )
        for group in loads:
            for copy in group:
                copy.start()
        for group, store in zip(loads, stores):
            for copy in group:
                copy.wait()
            store.start()
        for store in stores:
            store.wait()

    shape = (quads, rows, 2 * node + cols)
    return pl.pallas_call(
        body,
        in_specs=[pl.BlockSpec(memory_space=pl.ANY)] * 2,
        out_specs=pl.BlockSpec(memory_space=pl.ANY),
        out_shape=jax.ShapeDtypeStruct(shape, tokens.dtype),
        scratch_shapes=[
            pltpu.VMEM(shape, tokens.dtype),
            pltpu.SemaphoreType.DMA((quads, 2)),
            pltpu.SemaphoreType.DMA((quads,)),
            pltpu.SemaphoreType.DMA((quads,)),
        ],
        compiler_params=ALONE,
    )(tokens, grad_out)


def terms(packed, spot, part):
    sharers, rows, both = packed.shape
    cols = both - part
    wide = cols // 2
    step = 2
    steps = sharers // step

    def body(spot_ref, p_ref, keep_ref, send_ref, stage, sems):
        loads = []
        for k in range(steps):
            at = pl.ds(k * step, step)
            loads.append(
                pltpu.make_async_copy(p_ref.at[at], stage.at[at], sems.at[k])
            )
            loads[-1].start()
        first = spot_ref[0] == 0
        for k in range(steps):
            loads[k].wait()
            p = stage[k * step : (k + 1) * step].reshape(step * rows, both)
            left, right = p[:, part : part + wide], p[:, part + wide :]
            g = jnp.concatenate(
                [jnp.where(first, left, right), jnp.where(first, right, left)], axis=1
            )
            term = lax.dot_general(
                p[:, :part],
                g,
                (((0,), (0,)), ((), ())),
                preferred_element_type=jnp.float32,
            )
            if k == 0:
                keep_ref[...] = term[:, :wide]
                send_ref[...] = term[:, wide:]
            else:
                keep_ref[...] += term[:, :wide]
                send_ref[...] += term[:, wide:]

    half = jax.ShapeDtypeStruct((part, wide), jnp.float32)
    return pl.pallas_call(
        body,
        in_specs=[
            pl.BlockSpec(memory_space=pltpu.SMEM),
            pl.BlockSpec(memory_space=pl.ANY),
        ],
        out_specs=[pl.BlockSpec(memory_space=pltpu.VMEM)] * 2,
        out_shape=[half, half],
        scratch_shapes=[
            pltpu.VMEM(packed.shape, packed.dtype),
            pltpu.SemaphoreType.DMA((steps,)),
        ],
        compiler_params=PARAMS,
    )(spot, packed)


def join(parts):
    count = len(parts)

    def body(*refs):
        o_ref, sems = refs[count:]
        copies = [
            pltpu.make_async_copy(refs[n], o_ref.at[n], sems.at[n]) for n in range(count)
        ]
        for copy in copies:
            copy.start()
        for copy in copies:
            copy.wait()

    return pl.pallas_call(
        body,
        in_specs=[pl.BlockSpec(memory_space=pl.ANY)] * count,
        out_specs=pl.BlockSpec(memory_space=pltpu.VMEM),
        out_shape=jax.ShapeDtypeStruct((count,) + parts[0].shape, parts[0].dtype),
        scratch_shapes=[pltpu.SemaphoreType.DMA((count,))],
        compiler_params=PARAMS,
    )(*parts)


def project(packed, mine, other, spot):
    quads, rows, both = packed.shape
    pairs, zs, xhs, shard, wide = mine.shape
    depth = pairs * zs
    part, cols = depth * xhs * shard, 2 * wide

    def body(spot_ref, p_ref, m_ref, r_ref, near_ref, away_ref, stage, whole, sems):
        core, yl, xl, xh, z = (spot_ref[i] for i in range(5))
        loads = []
        for flip in range(quads):
            loads.append(
                pltpu.make_async_copy(
                    p_ref.at[(yl * 2 + xl) ^ flip], stage.at[flip], sems.at[flip]
                )
            )
            loads[-1].start()
        for back in range(pairs):
            at_z = lax.rem(z + depth - zs * back, depth)
            for slot in range(zs):
                for side in range(xhs):
                    ours, theirs = m_ref[back, slot, side], r_ref[back, slot, side]
                    left = jnp.where(core == 0, ours, theirs)
                    right = jnp.where(core == 0, theirs, ours)
                    whole[xh ^ side, at_z ^ slot] = jnp.concatenate(
                        [left, right], axis=1
                    )
        for load in loads:
            load.wait()
        t = stage[...].reshape(quads * rows, both)[:, :part]
        new = jnp.dot(
            t, whole[...].reshape(part, cols), preferred_element_type=jnp.float32
        ).reshape(quads, rows, cols)
        near_ref[...] = new[:2]
        away_ref[...] = new[2:]

    out = jax.ShapeDtypeStruct((2, rows, cols), jnp.float32)
    return pl.pallas_call(
        body,
        in_specs=[
            pl.BlockSpec(memory_space=pltpu.SMEM),
            pl.BlockSpec(memory_space=pl.ANY),
        ]
        + [pl.BlockSpec(memory_space=pltpu.VMEM)] * 2,
        out_specs=[pl.BlockSpec(memory_space=pltpu.VMEM)] * 2,
        out_shape=[out, out],
        scratch_shapes=[
            pltpu.VMEM(packed.shape, packed.dtype),
            pltpu.VMEM((xhs, depth, shard, cols), packed.dtype),
            pltpu.SemaphoreType.DMA((quads,)),
        ],
        compiler_params=PARAMS,
    )(spot, packed, mine, other)


def partners(sizes):
    yh, cores, yl, xh, xl = sizes
    lines, width = yh * yl, xh * xl

    def place(y, c, x):
        return ((((y // yl) * cores + c) * yl + y % yl) * xh + x // xl) * xl + x % xl

    def other(i, n, c):
        if c == 0:
            return i ^ 1
        return (i + 1) % n if i % 2 else (i - 1) % n

    flip_x, flip_y, squares = [], [], []
    for y in range(lines):
        for c in range(cores):
            for x in range(width):
                flip_x.append((place(y, c, x), place(y, c, other(x, width, c))))
                flip_y.append((place(y, c, x), place(other(y, lines, c), c, x)))
                if y % 2 == 0 and x % 2 == 0:
                    ys, xs = (y, other(y, lines, c)), (x, other(x, width, c))
                    squares.append([place(a, c, b) for a in ys for b in xs])
    return squares, flip_x, flip_y


def local(tokens, weight, grad_out):
    shard, cols = weight.shape
    wide = cols // 2
    depth = lax.axis_size("z")
    squares, flip_x, flip_y = partners([lax.axis_size(name) for name in CHIP])
    spot = jnp.stack([lax.axis_index(name) for name in ("c", "yl", "xl", "xh", "z")])
    spot = spot.astype(jnp.int32)

    mine = jnp.where(spot[0] == 0, weight[:, :wide], weight[:, wide:])
    pair = [(i, i ^ 1) for i in range(depth)]
    mine = jnp.stack([mine, lax.ppermute(mine, "xh", SWAP)])
    packed = pack(tokens, grad_out)
    packed, mine = lax.optimization_barrier((packed, mine))
    packed = lax.all_to_all(packed, CHIP, 0, 0, axis_index_groups=squares)
    part = packed.shape[-1] - cols
    mine = jnp.stack([mine, lax.ppermute(mine, "z", pair)])
    gathered = [mine]
    for back in range(2, depth, 2):
        shift = [(i, (i + back) % depth) for i in range(depth)]
        gathered.append(lax.ppermute(mine, "z", shift))
    packed, *gathered = lax.optimization_barrier((packed, *gathered))

    keep, send = terms(packed, spot, part)
    term = (keep + lax.ppermute(send, "c", SWAP)).astype(jnp.bfloat16)
    mine = join(gathered)
    mine, _ = lax.optimization_barrier((mine, send))
    other = lax.ppermute(mine, "c", SWAP)
    term = lax.all_to_all(term.reshape(-1, shard, wide), ("xh", "z"), 0, 0)
    summed = jnp.sum(term, axis=0, dtype=jnp.float32)

    near, away = project(packed, mine, other, spot)
    away = lax.ppermute(away, CHIP, flip_y)
    near, _ = lax.optimization_barrier((near, summed))
    near = near + away
    output = near[0] + lax.ppermute(near[1], CHIP, flip_x)

    lines = jnp.broadcast_to(summed[None], (lax.axis_size("yh"), shard, wide))
    half = jnp.sum(lax.all_to_all(lines, "yh", 0, 0), axis=0)
    other = lax.ppermute(half, "c", SWAP)
    first = spot[0] == 0
    weight_grad = jnp.concatenate(
        [jnp.where(first, half, other), jnp.where(first, other, half)], axis=1
    )
    return output.astype(jnp.bfloat16), weight_grad


def solution(mesh):
    inner = Mesh(
        mesh.devices.reshape(4, 2, 2, 2, 2, 8), ("yh", "c", "yl", "xh", "xl", "z")
    )
    rows = P(("yh", "c", "yl", "xh", "xl", "z"), None)
    owners = P(("yl", "xh", "xl", "z"), None)
    return jax.shard_map(
        local,
        mesh=inner,
        in_specs=(rows, owners, rows),
        out_specs=(rows, owners),
        check_vma=False,
    )
```

```python
import jax
import jax.numpy as jnp
from jax import lax
from jax.experimental import pallas as pl
from jax.experimental.pallas import tpu as pltpu
from jax.sharding import Mesh, PartitionSpec as P

PARAMS = pltpu.CompilerParams(vmem_limit_bytes=32 * 1024 * 1024)
ALONE = pltpu.CompilerParams(vmem_limit_bytes=60 * 1024 * 1024)
SWAP = [(0, 1), (1, 0)]
CHIP = ("yh", "c", "yl", "xh", "xl")


def pack(tokens, grad_out):
    rows, width = tokens.shape
    cols = grad_out.shape[1]
    quads, node = 4, width // 8

    def body(t_ref, g_ref, o_ref, stage, t_sems, g_sems, o_sems):
        loads, stores = [], []
        for quad in range(quads):
            group = []
            for xh in range(2):
                at = ((quad // 2) * 4 + xh * 2 + quad % 2) * node
                group.append(
                    pltpu.make_async_copy(
                        t_ref.at[:, pl.ds(at, node)],
                        stage.at[quad, :, pl.ds(xh * node, node)],
                        t_sems.at[quad, xh],
                    )
                )
            group.append(
                pltpu.make_async_copy(
                    g_ref, stage.at[quad, :, pl.ds(2 * node, cols)], g_sems.at[quad]
                )
            )
            loads.append(group)
            stores.append(
                pltpu.make_async_copy(stage.at[quad], o_ref.at[quad], o_sems.at[quad])
            )
        for group in loads:
            for copy in group:
                copy.start()
        for group, store in zip(loads, stores):
            for copy in group:
                copy.wait()
            store.start()
        for store in stores:
            store.wait()

    shape = (quads, rows, 2 * node + cols)
    return pl.pallas_call(
        body,
        in_specs=[pl.BlockSpec(memory_space=pl.ANY)] * 2,
        out_specs=pl.BlockSpec(memory_space=pl.ANY),
        out_shape=jax.ShapeDtypeStruct(shape, tokens.dtype),
        scratch_shapes=[
            pltpu.VMEM(shape, tokens.dtype),
            pltpu.SemaphoreType.DMA((quads, 2)),
            pltpu.SemaphoreType.DMA((quads,)),
            pltpu.SemaphoreType.DMA((quads,)),
        ],
        compiler_params=ALONE,
    )(tokens, grad_out)


def terms(packed, spot, part):
    sharers, rows, both = packed.shape
    cols = both - part
    wide = cols // 2
    step = 2
    steps = sharers // step

    def body(spot_ref, p_ref, keep_ref, send_ref, stage, sems):
        loads = []
        for k in range(steps):
            at = pl.ds(k * step, step)
            loads.append(
                pltpu.make_async_copy(p_ref.at[at], stage.at[at], sems.at[k])
            )
            loads[-1].start()
        first = spot_ref[0] == 0
        for k in range(steps):
            loads[k].wait()
            p = stage[k * step : (k + 1) * step].reshape(step * rows, both)
            left, right = p[:, part : part + wide], p[:, part + wide :]
            g = jnp.concatenate(
                [jnp.where(first, left, right), jnp.where(first, right, left)], axis=1
            )
            term = lax.dot_general(
                p[:, :part],
                g,
                (((0,), (0,)), ((), ())),
                preferred_element_type=jnp.float32,
            )
            if k == 0:
                keep_ref[...] = term[:, :wide]
                send_ref[...] = term[:, wide:]
            else:
                keep_ref[...] += term[:, :wide]
                send_ref[...] += term[:, wide:]

    half = jax.ShapeDtypeStruct((part, wide), jnp.float32)
    return pl.pallas_call(
        body,
        in_specs=[
            pl.BlockSpec(memory_space=pltpu.SMEM),
            pl.BlockSpec(memory_space=pl.ANY),
        ],
        out_specs=[pl.BlockSpec(memory_space=pltpu.VMEM)] * 2,
        out_shape=[half, half],
        scratch_shapes=[
            pltpu.VMEM(packed.shape, packed.dtype),
            pltpu.SemaphoreType.DMA((steps,)),
        ],
        compiler_params=PARAMS,
    )(spot, packed)


def project(packed, mine, other, spot):
    quads, rows, both = packed.shape
    depth, xhs, shard, wide = mine.shape
    part, cols = depth * xhs * shard, 2 * wide

    def body(spot_ref, p_ref, m_ref, r_ref, near_ref, away_ref, stage, whole, sems):
        core, yl, xl, xh = (spot_ref[i] for i in range(4))
        loads = []
        for flip in range(quads):
            loads.append(
                pltpu.make_async_copy(
                    p_ref.at[(yl * 2 + xl) ^ flip], stage.at[flip], sems.at[flip]
                )
            )
            loads[-1].start()
        for z in range(depth):
            for side in range(xhs):
                ours, theirs = m_ref[z, side], r_ref[z, side]
                left = jnp.where(core == 0, ours, theirs)
                right = jnp.where(core == 0, theirs, ours)
                whole[xh ^ side, z] = jnp.concatenate([left, right], axis=1)
        for load in loads:
            load.wait()
        t = stage[...].reshape(quads * rows, both)[:, :part]
        new = jnp.dot(
            t, whole[...].reshape(part, cols), preferred_element_type=jnp.float32
        ).reshape(quads, rows, cols)
        near_ref[...] = new[:2]
        away_ref[...] = new[2:]

    out = jax.ShapeDtypeStruct((2, rows, cols), jnp.float32)
    return pl.pallas_call(
        body,
        in_specs=[
            pl.BlockSpec(memory_space=pltpu.SMEM),
            pl.BlockSpec(memory_space=pl.ANY),
        ]
        + [pl.BlockSpec(memory_space=pltpu.VMEM)] * 2,
        out_specs=[pl.BlockSpec(memory_space=pltpu.VMEM)] * 2,
        out_shape=[out, out],
        scratch_shapes=[
            pltpu.VMEM(packed.shape, packed.dtype),
            pltpu.VMEM((xhs, depth, shard, cols), packed.dtype),
            pltpu.SemaphoreType.DMA((quads,)),
        ],
        compiler_params=PARAMS,
    )(spot, packed, mine, other)


def partners(sizes):
    yh, cores, yl, xh, xl = sizes
    lines, width = yh * yl, xh * xl

    def place(y, c, x):
        return ((((y // yl) * cores + c) * yl + y % yl) * xh + x // xl) * xl + x % xl

    def other(i, n, c):
        if c == 0:
            return i ^ 1
        return (i + 1) % n if i % 2 else (i - 1) % n

    flip_x, flip_y, squares = [], [], []
    for y in range(lines):
        for c in range(cores):
            for x in range(width):
                flip_x.append((place(y, c, x), place(y, c, other(x, width, c))))
                flip_y.append((place(y, c, x), place(other(y, lines, c), c, x)))
                if y % 2 == 0 and x % 2 == 0:
                    ys, xs = (y, other(y, lines, c)), (x, other(x, width, c))
                    squares.append([place(a, c, b) for a in ys for b in xs])
    return squares, flip_x, flip_y


def local(tokens, weight, grad_out):
    shard, cols = weight.shape
    wide = cols // 2
    squares, flip_x, flip_y = partners([lax.axis_size(name) for name in CHIP])
    spot = jnp.stack([lax.axis_index(name) for name in ("c", "yl", "xl", "xh")])
    spot = spot.astype(jnp.int32)

    other = lax.ppermute(weight, "xh", SWAP)
    packed = pack(tokens, grad_out)
    packed, other = lax.optimization_barrier((packed, other))
    packed = lax.all_to_all(packed, CHIP, 0, 0, axis_index_groups=squares)
    part = packed.shape[-1] - cols
    mine = jnp.stack([weight, other])
    mine = jnp.where(spot[0] == 0, mine[..., :wide], mine[..., wide:])
    mine = lax.all_gather(mine, "z", axis=0)
    packed, mine = lax.optimization_barrier((packed, mine))

    keep, send = terms(packed, spot, part)
    term = (keep + lax.ppermute(send, "c", SWAP)).astype(jnp.bfloat16)
    mine, _ = lax.optimization_barrier((mine, send))
    other = lax.ppermute(mine, "c", SWAP)
    term = lax.all_to_all(term.reshape(-1, shard, wide), ("xh", "z"), 0, 0)
    summed = jnp.sum(term, axis=0, dtype=jnp.float32)

    near, away = project(packed, mine, other, spot)
    away = lax.ppermute(away, CHIP, flip_y)
    near, _ = lax.optimization_barrier((near, summed))
    near = near + away
    output = near[0] + lax.ppermute(near[1], CHIP, flip_x)

    lines = jnp.broadcast_to(summed[None], (lax.axis_size("yh"), shard, wide))
    half = jnp.sum(lax.all_to_all(lines, "yh", 0, 0), axis=0)
    other = lax.ppermute(half, "c", SWAP)
    first = spot[0] == 0
    weight_grad = jnp.concatenate(
        [jnp.where(first, half, other), jnp.where(first, other, half)], axis=1
    )
    return output.astype(jnp.bfloat16), weight_grad


def solution(mesh):
    inner = Mesh(
        mesh.devices.reshape(4, 2, 2, 2, 2, 8), ("yh", "c", "yl", "xh", "xl", "z")
    )
    rows = P(("yh", "c", "yl", "xh", "xl", "z"), None)
    owners = P(("yl", "xh", "xl", "z"), None)
    return jax.shard_map(
        local,
        mesh=inner,
        in_specs=(rows, owners, rows),
        out_specs=(rows, owners),
        check_vma=False,
    )
```

```python
import jax
import jax.numpy as jnp
from jax import lax
from jax.experimental import pallas as pl
from jax.experimental.pallas import tpu as pltpu
from jax.sharding import Mesh, PartitionSpec as P

PARAMS = pltpu.CompilerParams(vmem_limit_bytes=32 * 1024 * 1024)
ALONE = pltpu.CompilerParams(vmem_limit_bytes=60 * 1024 * 1024)
SWAP = [(0, 1), (1, 0)]
CHIP = ("yh", "c", "yl", "xh", "xl", "zh", "zl")


def pack(tokens, grad_out, shard):
    rows, width = tokens.shape
    cols = grad_out.shape[1]
    node = width // 8
    part = width // 8

    def body(t_ref, g_ref, o_ref, held, stage, t_sems, g_sems, o_sems):
        loads, sides, stores = [], [], []
        for quad in range(4):
            for xh in range(2):
                at = ((quad // 2) * 4 + xh * 2 + quad % 2) * node
                copy = pltpu.make_async_copy(
                    t_ref.at[:, pl.ds(at, node)],
                    held.at[quad * 2 + xh],
                    t_sems.at[quad * 2 + xh],
                )
                copy.start()
                loads.append(copy)
        for o in range(8):
            copy = pltpu.make_async_copy(
                g_ref, stage.at[o, :, pl.ds(part, cols)], g_sems.at[o]
            )
            copy.start()
            sides.append(copy)
        for quad in range(4):
            for xh in range(2):
                loads[quad * 2 + xh].wait()
                t = held[quad * 2 + xh]
                for zl in range(2):
                    pieces = [
                        t[:, at : at + shard]
                        for at in range(zl * shard, node, 2 * shard)
                    ]
                    stage[quad * 2 + zl, :, xh * node // 2 : (xh + 1) * node // 2] = (
                        jnp.concatenate(pieces, axis=1)
                    )
            for zl in range(2):
                o = quad * 2 + zl
                sides[o].wait()
                copy = pltpu.make_async_copy(stage.at[o], o_ref.at[o], o_sems.at[o])
                copy.start()
                stores.append(copy)
        for copy in stores:
            copy.wait()

    shape = (8, rows, part + cols)
    return pl.pallas_call(
        body,
        in_specs=[pl.BlockSpec(memory_space=pl.ANY)] * 2,
        out_specs=pl.BlockSpec(memory_space=pl.ANY),
        out_shape=jax.ShapeDtypeStruct(shape, tokens.dtype),
        scratch_shapes=[
            pltpu.VMEM((8, rows, node), tokens.dtype),
            pltpu.VMEM(shape, tokens.dtype),
        ]
        + [pltpu.SemaphoreType.DMA((8,))] * 3,
        compiler_params=ALONE,
    )(tokens, grad_out)


def terms(packed, spot, part):
    sharers, rows, both = packed.shape
    cols = both - part
    wide = cols // 2
    step = 2
    steps = sharers // step

    def body(spot_ref, p_ref, keep_ref, send_ref, stage, sems):
        loads = []
        for k in range(steps):
            at = pl.ds(k * step, step)
            loads.append(
                pltpu.make_async_copy(p_ref.at[at], stage.at[at], sems.at[k])
            )
            loads[-1].start()
        first = spot_ref[0] == 0
        for k in range(steps):
            loads[k].wait()
            p = stage[k * step : (k + 1) * step].reshape(step * rows, both)
            left, right = p[:, part : part + wide], p[:, part + wide :]
            g = jnp.concatenate(
                [jnp.where(first, left, right), jnp.where(first, right, left)], axis=1
            )
            term = lax.dot_general(
                p[:, :part],
                g,
                (((0,), (0,)), ((), ())),
                preferred_element_type=jnp.float32,
            )
            if k == 0:
                keep_ref[...] = term[:, :wide]
                send_ref[...] = term[:, wide:]
            else:
                keep_ref[...] += term[:, :wide]
                send_ref[...] += term[:, wide:]

    half = jax.ShapeDtypeStruct((part, wide), jnp.float32)
    return pl.pallas_call(
        body,
        in_specs=[
            pl.BlockSpec(memory_space=pltpu.SMEM),
            pl.BlockSpec(memory_space=pl.ANY),
        ],
        out_specs=[pl.BlockSpec(memory_space=pltpu.VMEM)] * 2,
        out_shape=[half, half],
        scratch_shapes=[
            pltpu.VMEM(packed.shape, packed.dtype),
            pltpu.SemaphoreType.DMA((steps,)),
        ],
        compiler_params=PARAMS,
    )(spot, packed)


def project(packed, mine, other, spot):
    sharers, rows, both = packed.shape
    depth, xhs, shard, wide = mine.shape
    part, cols = depth * xhs * shard, 2 * wide

    def body(spot_ref, p_ref, m_ref, r_ref, near_ref, away_ref, stage, whole, sems):
        core, yl, xl, zl, xh = (spot_ref[i] for i in range(5))
        own = (yl * 2 + xl) * 2 + zl
        loads = []
        for flip in range(sharers):
            loads.append(
                pltpu.make_async_copy(
                    p_ref.at[own ^ flip], stage.at[flip], sems.at[flip]
                )
            )
            loads[-1].start()
        for z in range(depth):
            for side in range(xhs):
                ours, theirs = m_ref[z, side], r_ref[z, side]
                left = jnp.where(core == 0, ours, theirs)
                right = jnp.where(core == 0, theirs, ours)
                whole[xh ^ side, z] = jnp.concatenate([left, right], axis=1)
        for load in loads:
            load.wait()
        t = stage[...].reshape(sharers * rows, both)[:, :part]
        new = jnp.dot(
            t, whole[...].reshape(part, cols), preferred_element_type=jnp.float32
        ).reshape(sharers, rows, cols)
        near_ref[...] = new[: sharers // 2]
        away_ref[...] = new[sharers // 2 :]

    out = jax.ShapeDtypeStruct((sharers // 2, rows, cols), jnp.float32)
    return pl.pallas_call(
        body,
        in_specs=[
            pl.BlockSpec(memory_space=pltpu.SMEM),
            pl.BlockSpec(memory_space=pl.ANY),
        ]
        + [pl.BlockSpec(memory_space=pltpu.VMEM)] * 2,
        out_specs=[pl.BlockSpec(memory_space=pltpu.VMEM)] * 2,
        out_shape=[out, out],
        scratch_shapes=[
            pltpu.VMEM(packed.shape, packed.dtype),
            pltpu.VMEM((xhs, depth, shard, cols), packed.dtype),
            pltpu.SemaphoreType.DMA((sharers,)),
        ],
        compiler_params=PARAMS,
    )(spot, packed, mine, other)


def partners(sizes):
    yh, cores, yl, xh, xl, zh, zl = sizes
    rings = (yh * yl, xh * xl, zh * zl)

    def place(c, y, x, z):
        at = ((y // yl) * cores + c) * yl + y % yl
        return (at * xh * xl + x) * zh * zl + z

    def other(i, n, c):
        if c == 0:
            return i ^ 1
        return (i + 1) % n if i % 2 else (i - 1) % n

    flips, cubes = ([], [], []), []
    for c in range(cores):
        for y in range(rings[0]):
            for x in range(rings[1]):
                for z in range(rings[2]):
                    here = (y, x, z)
                    there = [other(i, n, c) for i, n in zip(here, rings)]
                    for axis in range(3):
                        to = list(here)
                        to[axis] = there[axis]
                        flips[axis].append((place(c, *here), place(c, *to)))
                    if all(i % 2 == 0 for i in here):
                        pairs = list(zip(here, there))
                        cubes.append(
                            [
                                place(c, a, b, d)
                                for a in pairs[0]
                                for b in pairs[1]
                                for d in pairs[2]
                            ]
                        )
    return cubes, *flips


def local(tokens, weight, grad_out):
    shard, cols = weight.shape
    wide = cols // 2
    cubes, flip_y, flip_x, flip_z = partners([lax.axis_size(name) for name in CHIP])
    spot = jnp.stack([lax.axis_index(name) for name in ("c", "yl", "xl", "zl", "xh")])
    spot = spot.astype(jnp.int32)

    other = lax.ppermute(weight, "xh", SWAP)
    packed = pack(tokens, grad_out, shard)
    packed, other = lax.optimization_barrier((packed, other))
    packed = lax.all_to_all(packed, CHIP, 0, 0, axis_index_groups=cubes)
    part = packed.shape[-1] - cols
    mine = jnp.stack([weight, other])
    mine = jnp.where(spot[0] == 0, mine[..., :wide], mine[..., wide:])
    mine = lax.all_gather(mine, "zh", axis=0)
    packed, mine = lax.optimization_barrier((packed, mine))

    keep, send = terms(packed, spot, part)
    term = (keep + lax.ppermute(send, "c", SWAP)).astype(jnp.bfloat16)
    mine, _ = lax.optimization_barrier((mine, send))
    other = lax.ppermute(mine, "c", SWAP)
    term = lax.all_to_all(term.reshape(-1, shard, wide), ("xh", "zh"), 0, 0)
    summed = jnp.sum(term, axis=0, dtype=jnp.float32)

    near, away = project(packed, mine, other, spot)
    away = lax.ppermute(away, CHIP, flip_y)
    near, _ = lax.optimization_barrier((near, summed))
    near = near + away
    near = near[:2] + lax.ppermute(near[2:], CHIP, flip_x)

    lines = jnp.broadcast_to(summed[None], (lax.axis_size("yh"), shard, wide))
    half = jnp.sum(lax.all_to_all(lines, "yh", 0, 0), axis=0)
    other = lax.ppermute(half, "c", SWAP)
    near, _ = lax.optimization_barrier((near, half))
    output = near[0] + lax.ppermute(near[1], CHIP, flip_z)
    first = spot[0] == 0
    weight_grad = jnp.concatenate(
        [jnp.where(first, half, other), jnp.where(first, other, half)], axis=1
    )
    return output.astype(jnp.bfloat16), weight_grad


def solution(mesh):
    inner = Mesh(mesh.devices.reshape(4, 2, 2, 2, 2, 4, 2), CHIP)
    rows = P(CHIP, None)
    owners = P(("yl", "xh", "xl", "zh", "zl"), None)
    return jax.shard_map(
        local,
        mesh=inner,
        in_specs=(rows, owners, rows),
        out_specs=(rows, owners),
        check_vma=False,
    )
```

```python
import jax
import jax.numpy as jnp
from jax import lax
from jax.experimental import pallas as pl
from jax.experimental.pallas import tpu as pltpu
from jax.sharding import Mesh, PartitionSpec as P

PARAMS = pltpu.CompilerParams(vmem_limit_bytes=32 * 1024 * 1024)
ALONE = pltpu.CompilerParams(vmem_limit_bytes=60 * 1024 * 1024)
SWAP = [(0, 1), (1, 0)]
CHIP = ("yh", "c", "yl", "xh", "xl", "zh", "zl")


def pack(tokens, grad_out, shard):
    rows, width = tokens.shape
    cols = grad_out.shape[1]
    node = width // 8
    part = width // 8

    def body(t_ref, g_ref, o_ref, held, stage, t_sems, g_sems, o_sems):
        loads, sides, stores = [], [], []
        for quad in range(4):
            for xh in range(2):
                at = ((quad // 2) * 4 + xh * 2 + quad % 2) * node
                copy = pltpu.make_async_copy(
                    t_ref.at[:, pl.ds(at, node)],
                    held.at[quad * 2 + xh],
                    t_sems.at[quad * 2 + xh],
                )
                copy.start()
                loads.append(copy)
        for o in range(8):
            copy = pltpu.make_async_copy(
                g_ref, stage.at[o, :, pl.ds(part, cols)], g_sems.at[o]
            )
            copy.start()
            sides.append(copy)
        for quad in range(4):
            for xh in range(2):
                loads[quad * 2 + xh].wait()
                t = held[quad * 2 + xh]
                for zl in range(2):
                    pieces = [
                        t[:, at : at + shard]
                        for at in range(zl * shard, node, 2 * shard)
                    ]
                    stage[quad * 2 + zl, :, xh * node // 2 : (xh + 1) * node // 2] = (
                        jnp.concatenate(pieces, axis=1)
                    )
            for zl in range(2):
                o = quad * 2 + zl
                sides[o].wait()
                copy = pltpu.make_async_copy(stage.at[o], o_ref.at[o], o_sems.at[o])
                copy.start()
                stores.append(copy)
        for copy in stores:
            copy.wait()

    shape = (8, rows, part + cols)
    return pl.pallas_call(
        body,
        in_specs=[pl.BlockSpec(memory_space=pl.ANY)] * 2,
        out_specs=pl.BlockSpec(memory_space=pl.ANY),
        out_shape=jax.ShapeDtypeStruct(shape, tokens.dtype),
        scratch_shapes=[
            pltpu.VMEM((8, rows, node), tokens.dtype),
            pltpu.VMEM(shape, tokens.dtype),
        ]
        + [pltpu.SemaphoreType.DMA((8,))] * 3,
        compiler_params=ALONE,
    )(tokens, grad_out)


def terms(packed, spot, part):
    sharers, rows, both = packed.shape
    cols = both - part
    wide = cols // 2
    step = 2
    steps = sharers // step

    def body(spot_ref, p_ref, keep_ref, send_ref, stage, sems):
        loads = []
        for k in range(steps):
            at = pl.ds(k * step, step)
            loads.append(
                pltpu.make_async_copy(p_ref.at[at], stage.at[at], sems.at[k])
            )
            loads[-1].start()
        first = spot_ref[0] == 0
        for k in range(steps):
            loads[k].wait()
            p = stage[k * step : (k + 1) * step].reshape(step * rows, both)
            left, right = p[:, part : part + wide], p[:, part + wide :]
            g = jnp.concatenate(
                [jnp.where(first, left, right), jnp.where(first, right, left)], axis=1
            )
            term = lax.dot_general(
                p[:, :part],
                g,
                (((0,), (0,)), ((), ())),
                preferred_element_type=jnp.float32,
            )
            if k == 0:
                keep_ref[...] = term[:, :wide]
                send_ref[...] = term[:, wide:]
            else:
                keep_ref[...] += term[:, :wide]
                send_ref[...] += term[:, wide:]

    half = jax.ShapeDtypeStruct((part, wide), jnp.float32)
    return pl.pallas_call(
        body,
        in_specs=[
            pl.BlockSpec(memory_space=pltpu.SMEM),
            pl.BlockSpec(memory_space=pl.ANY),
        ],
        out_specs=[pl.BlockSpec(memory_space=pltpu.VMEM)] * 2,
        out_shape=[half, half],
        scratch_shapes=[
            pltpu.VMEM(packed.shape, packed.dtype),
            pltpu.SemaphoreType.DMA((steps,)),
        ],
        compiler_params=PARAMS,
    )(spot, packed)


def join(parts):
    count = len(parts)

    def body(*refs):
        o_ref, sems = refs[count:]
        copies = [
            pltpu.make_async_copy(refs[n], o_ref.at[n], sems.at[n]) for n in range(count)
        ]
        for copy in copies:
            copy.start()
        for copy in copies:
            copy.wait()

    return pl.pallas_call(
        body,
        in_specs=[pl.BlockSpec(memory_space=pl.ANY)] * count,
        out_specs=pl.BlockSpec(memory_space=pltpu.VMEM),
        out_shape=jax.ShapeDtypeStruct((count,) + parts[0].shape, parts[0].dtype),
        scratch_shapes=[pltpu.SemaphoreType.DMA((count,))],
        compiler_params=PARAMS,
    )(*parts)


def project(packed, mine, other, spot):
    sharers, rows, both = packed.shape
    depth, xhs, shard, wide = mine.shape
    part, cols = depth * xhs * shard, 2 * wide

    def body(spot_ref, p_ref, m_ref, r_ref, near_ref, away_ref, stage, whole, sems):
        core, yl, xl, zl, xh, zh = (spot_ref[i] for i in range(6))
        own = (yl * 2 + xl) * 2 + zl
        loads = []
        for flip in range(sharers):
            loads.append(
                pltpu.make_async_copy(
                    p_ref.at[own ^ flip], stage.at[flip], sems.at[flip]
                )
            )
            loads[-1].start()
        for back in range(depth):
            at_z = lax.rem(zh + depth - back, depth)
            for side in range(xhs):
                ours, theirs = m_ref[back, side], r_ref[back, side]
                left = jnp.where(core == 0, ours, theirs)
                right = jnp.where(core == 0, theirs, ours)
                whole[xh ^ side, at_z] = jnp.concatenate([left, right], axis=1)
        for load in loads:
            load.wait()
        t = stage[...].reshape(sharers * rows, both)[:, :part]
        new = jnp.dot(
            t, whole[...].reshape(part, cols), preferred_element_type=jnp.float32
        ).reshape(sharers, rows, cols)
        near_ref[...] = new[: sharers // 2]
        away_ref[...] = new[sharers // 2 :]

    out = jax.ShapeDtypeStruct((sharers // 2, rows, cols), jnp.float32)
    return pl.pallas_call(
        body,
        in_specs=[
            pl.BlockSpec(memory_space=pltpu.SMEM),
            pl.BlockSpec(memory_space=pl.ANY),
        ]
        + [pl.BlockSpec(memory_space=pltpu.VMEM)] * 2,
        out_specs=[pl.BlockSpec(memory_space=pltpu.VMEM)] * 2,
        out_shape=[out, out],
        scratch_shapes=[
            pltpu.VMEM(packed.shape, packed.dtype),
            pltpu.VMEM((xhs, depth, shard, cols), packed.dtype),
            pltpu.SemaphoreType.DMA((sharers,)),
        ],
        compiler_params=PARAMS,
    )(spot, packed, mine, other)


def partners(sizes):
    yh, cores, yl, xh, xl, zh, zl = sizes
    rings = (yh * yl, xh * xl, zh * zl)

    def place(c, y, x, z):
        at = ((y // yl) * cores + c) * yl + y % yl
        return (at * xh * xl + x) * zh * zl + z

    def other(i, n, c):
        if c == 0:
            return i ^ 1
        return (i + 1) % n if i % 2 else (i - 1) % n

    flips, cubes = ([], [], []), []
    for c in range(cores):
        for y in range(rings[0]):
            for x in range(rings[1]):
                for z in range(rings[2]):
                    here = (y, x, z)
                    there = [other(i, n, c) for i, n in zip(here, rings)]
                    for axis in range(3):
                        to = list(here)
                        to[axis] = there[axis]
                        flips[axis].append((place(c, *here), place(c, *to)))
                    if all(i % 2 == 0 for i in here):
                        pairs = list(zip(here, there))
                        cubes.append(
                            [
                                place(c, a, b, d)
                                for a in pairs[0]
                                for b in pairs[1]
                                for d in pairs[2]
                            ]
                        )
    return cubes, *flips


def local(tokens, weight, grad_out):
    shard, cols = weight.shape
    wide = cols // 2
    cubes, flip_y, flip_x, flip_z = partners([lax.axis_size(name) for name in CHIP])
    here = ("c", "yl", "xl", "zl", "xh", "zh")
    spot = jnp.stack([lax.axis_index(name) for name in here])
    spot = spot.astype(jnp.int32)

    other = lax.ppermute(weight, "xh", SWAP)
    packed = pack(tokens, grad_out, shard)
    packed, other = lax.optimization_barrier((packed, other))
    packed = lax.all_to_all(packed, CHIP, 0, 0, axis_index_groups=cubes)
    part = packed.shape[-1] - cols
    mine = jnp.stack([weight, other])
    mine = jnp.where(spot[0] == 0, mine[..., :wide], mine[..., wide:])
    depth = lax.axis_size("zh")
    gathered = [mine]
    for back in range(1, depth):
        shift = [(i, (i + back) % depth) for i in range(depth)]
        gathered.append(lax.ppermute(mine, "zh", shift))
    packed, *gathered = lax.optimization_barrier((packed, *gathered))

    keep, send = terms(packed, spot, part)
    term = (keep + lax.ppermute(send, "c", SWAP)).astype(jnp.bfloat16)
    mine, _ = lax.optimization_barrier((join(gathered), send))
    other = lax.ppermute(mine, "c", SWAP)
    term = lax.all_to_all(term.reshape(-1, shard, wide), ("xh", "zh"), 0, 0)
    summed = jnp.sum(term, axis=0, dtype=jnp.float32)

    near, away = project(packed, mine, other, spot)
    away = lax.ppermute(away, CHIP, flip_y)
    near, _ = lax.optimization_barrier((near, summed))
    near = near + away
    near = near[:2] + lax.ppermute(near[2:], CHIP, flip_x)

    lines = jnp.broadcast_to(summed[None], (lax.axis_size("yh"), shard, wide))
    lines = lax.all_to_all(lines, "yh", 0, 0)
    near, lines = lax.optimization_barrier((near, lines))
    half = jnp.sum(lines, axis=0)
    other = lax.ppermute(half, "c", SWAP)
    output = near[0] + lax.ppermute(near[1], CHIP, flip_z)
    first = spot[0] == 0
    weight_grad = jnp.concatenate(
        [jnp.where(first, half, other), jnp.where(first, other, half)], axis=1
    )
    return output.astype(jnp.bfloat16), weight_grad


def solution(mesh):
    inner = Mesh(mesh.devices.reshape(4, 2, 2, 2, 2, 4, 2), CHIP)
    rows = P(CHIP, None)
    owners = P(("yl", "xh", "xl", "zh", "zl"), None)
    return jax.shard_map(
        local,
        mesh=inner,
        in_specs=(rows, owners, rows),
        out_specs=(rows, owners),
        check_vma=False,
    )
```

```python
import jax
import jax.numpy as jnp
from jax import lax
from jax.experimental import pallas as pl
from jax.experimental.pallas import tpu as pltpu
from jax.sharding import Mesh, PartitionSpec as P

PARAMS = pltpu.CompilerParams(vmem_limit_bytes=32 * 1024 * 1024)
ALONE = pltpu.CompilerParams(vmem_limit_bytes=60 * 1024 * 1024)
SWAP = [(0, 1), (1, 0)]
CHIP = ("yh", "c", "yl", "xh", "xl", "zh", "zl")


def pack(tokens, grad_out, shard):
    rows, width = tokens.shape
    cols = grad_out.shape[1]
    node = width // 8
    part = width // 8

    def body(t_ref, g_ref, o_ref, held, stage, t_sems, g_sems, o_sems):
        loads, sides, stores = [], [], []
        for quad in range(4):
            for xh in range(2):
                at = ((quad // 2) * 4 + xh * 2 + quad % 2) * node
                copy = pltpu.make_async_copy(
                    t_ref.at[:, pl.ds(at, node)],
                    held.at[quad * 2 + xh],
                    t_sems.at[quad * 2 + xh],
                )
                copy.start()
                loads.append(copy)
        for o in range(8):
            copy = pltpu.make_async_copy(
                g_ref, stage.at[o, :, pl.ds(part, cols)], g_sems.at[o]
            )
            copy.start()
            sides.append(copy)
        for quad in range(4):
            for xh in range(2):
                loads[quad * 2 + xh].wait()
                t = held[quad * 2 + xh]
                for zl in range(2):
                    pieces = [
                        t[:, at : at + shard]
                        for at in range(zl * shard, node, 2 * shard)
                    ]
                    stage[quad * 2 + zl, :, xh * node // 2 : (xh + 1) * node // 2] = (
                        jnp.concatenate(pieces, axis=1)
                    )
            for zl in range(2):
                o = quad * 2 + zl
                sides[o].wait()
                copy = pltpu.make_async_copy(stage.at[o], o_ref.at[o], o_sems.at[o])
                copy.start()
                stores.append(copy)
        for copy in stores:
            copy.wait()

    shape = (8, rows, part + cols)
    return pl.pallas_call(
        body,
        in_specs=[pl.BlockSpec(memory_space=pl.ANY)] * 2,
        out_specs=pl.BlockSpec(memory_space=pl.ANY),
        out_shape=jax.ShapeDtypeStruct(shape, tokens.dtype),
        scratch_shapes=[
            pltpu.VMEM((8, rows, node), tokens.dtype),
            pltpu.VMEM(shape, tokens.dtype),
        ]
        + [pltpu.SemaphoreType.DMA((8,))] * 3,
        compiler_params=ALONE,
    )(tokens, grad_out)


def terms(packed, spot, part):
    sharers, rows, both = packed.shape
    cols = both - part
    wide = cols // 2
    step = 2
    steps = sharers // step

    def body(spot_ref, p_ref, keep_ref, send_ref, stage, sems):
        loads = []
        for k in range(steps):
            at = pl.ds(k * step, step)
            loads.append(
                pltpu.make_async_copy(p_ref.at[at], stage.at[at], sems.at[k])
            )
            loads[-1].start()
        first = spot_ref[0] == 0
        for k in range(steps):
            loads[k].wait()
            p = stage[k * step : (k + 1) * step].reshape(step * rows, both)
            left, right = p[:, part : part + wide], p[:, part + wide :]
            g = jnp.concatenate(
                [jnp.where(first, left, right), jnp.where(first, right, left)], axis=1
            )
            term = lax.dot_general(
                p[:, :part],
                g,
                (((0,), (0,)), ((), ())),
                preferred_element_type=jnp.float32,
            )
            if k == 0:
                keep_ref[...] = term[:, :wide]
                send_ref[...] = term[:, wide:]
            else:
                keep_ref[...] += term[:, :wide]
                send_ref[...] += term[:, wide:]

    half = jax.ShapeDtypeStruct((part, wide), jnp.float32)
    return pl.pallas_call(
        body,
        in_specs=[
            pl.BlockSpec(memory_space=pltpu.SMEM),
            pl.BlockSpec(memory_space=pl.ANY),
        ],
        out_specs=[pl.BlockSpec(memory_space=pltpu.VMEM)] * 2,
        out_shape=[half, half],
        scratch_shapes=[
            pltpu.VMEM(packed.shape, packed.dtype),
            pltpu.SemaphoreType.DMA((steps,)),
        ],
        compiler_params=PARAMS,
    )(spot, packed)


def join(parts):
    count = len(parts)

    def body(*refs):
        o_ref, sems = refs[count:]
        copies = [
            pltpu.make_async_copy(refs[n], o_ref.at[n], sems.at[n]) for n in range(count)
        ]
        for copy in copies:
            copy.start()
        for copy in copies:
            copy.wait()

    return pl.pallas_call(
        body,
        in_specs=[pl.BlockSpec(memory_space=pl.ANY)] * count,
        out_specs=pl.BlockSpec(memory_space=pltpu.VMEM),
        out_shape=jax.ShapeDtypeStruct((count,) + parts[0].shape, parts[0].dtype),
        scratch_shapes=[pltpu.SemaphoreType.DMA((count,))],
        compiler_params=PARAMS,
    )(*parts)


def project(packed, mine, other, spot):
    sharers, rows, both = packed.shape
    depth, xhs, shard, wide = mine.shape
    part, cols = depth * xhs * shard, 2 * wide

    def body(spot_ref, p_ref, m_ref, r_ref, near_ref, away_ref, stage, whole, sems):
        core, yl, xl, zl, xh, zh = (spot_ref[i] for i in range(6))
        own = (yl * 2 + xl) * 2 + zl
        loads = []
        for flip in range(sharers):
            loads.append(
                pltpu.make_async_copy(
                    p_ref.at[own ^ flip], stage.at[flip], sems.at[flip]
                )
            )
            loads[-1].start()
        for back in range(depth):
            at_z = lax.rem(zh + depth - back, depth)
            for side in range(xhs):
                ours, theirs = m_ref[back, side], r_ref[back, side]
                left = jnp.where(core == 0, ours, theirs)
                right = jnp.where(core == 0, theirs, ours)
                whole[xh ^ side, at_z] = jnp.concatenate([left, right], axis=1)
        for load in loads:
            load.wait()
        t = stage[...].reshape(sharers * rows, both)[:, :part]
        new = jnp.dot(
            t, whole[...].reshape(part, cols), preferred_element_type=jnp.float32
        ).reshape(sharers, rows, cols)
        near_ref[...] = new[: sharers // 2]
        away_ref[...] = new[sharers // 2 :]

    out = jax.ShapeDtypeStruct((sharers // 2, rows, cols), jnp.float32)
    return pl.pallas_call(
        body,
        in_specs=[
            pl.BlockSpec(memory_space=pltpu.SMEM),
            pl.BlockSpec(memory_space=pl.ANY),
        ]
        + [pl.BlockSpec(memory_space=pltpu.VMEM)] * 2,
        out_specs=[pl.BlockSpec(memory_space=pltpu.VMEM)] * 2,
        out_shape=[out, out],
        scratch_shapes=[
            pltpu.VMEM(packed.shape, packed.dtype),
            pltpu.VMEM((xhs, depth, shard, cols), packed.dtype),
            pltpu.SemaphoreType.DMA((sharers,)),
        ],
        compiler_params=PARAMS,
    )(spot, packed, mine, other)


def partners(sizes):
    yh, cores, yl, xh, xl, zh, zl = sizes
    rings = (yh * yl, xh * xl, zh * zl)

    def place(c, y, x, z):
        at = ((y // yl) * cores + c) * yl + y % yl
        return (at * xh * xl + x) * zh * zl + z

    def other(i, n, c):
        if c == 0:
            return i ^ 1
        return (i + 1) % n if i % 2 else (i - 1) % n

    moves = ((1, 0, 0), (0, 0, 1), (0, 1, 0), (0, 1, 1))
    flips, cubes = [[] for _ in moves], []
    for c in range(cores):
        for y in range(rings[0]):
            for x in range(rings[1]):
                for z in range(rings[2]):
                    here = (y, x, z)
                    there = [other(i, n, c) for i, n in zip(here, rings)]
                    for move, flip in zip(moves, flips):
                        to = [b if m else a for a, b, m in zip(here, there, move)]
                        flip.append((place(c, *here), place(c, *to)))
                    if all(i % 2 == 0 for i in here):
                        pairs = list(zip(here, there))
                        cubes.append(
                            [
                                place(c, a, b, d)
                                for a in pairs[0]
                                for b in pairs[1]
                                for d in pairs[2]
                            ]
                        )
    return cubes, flips[0], flips[1:]


def local(tokens, weight, grad_out):
    shard, cols = weight.shape
    wide = cols // 2
    cubes, flip_y, flips = partners([lax.axis_size(name) for name in CHIP])
    here = ("c", "yl", "xl", "zl", "xh", "zh")
    spot = jnp.stack([lax.axis_index(name) for name in here])
    spot = spot.astype(jnp.int32)

    other = lax.ppermute(weight, "xh", SWAP)
    packed = pack(tokens, grad_out, shard)
    packed, other = lax.optimization_barrier((packed, other))
    packed = lax.all_to_all(packed, CHIP, 0, 0, axis_index_groups=cubes)
    part = packed.shape[-1] - cols
    mine = jnp.stack([weight, other])
    mine = jnp.where(spot[0] == 0, mine[..., :wide], mine[..., wide:])
    depth = lax.axis_size("zh")
    gathered = [mine]
    for back in range(1, depth):
        shift = [(i, (i + back) % depth) for i in range(depth)]
        gathered.append(lax.ppermute(mine, "zh", shift))
    packed, *gathered = lax.optimization_barrier((packed, *gathered))

    keep, send = terms(packed, spot, part)
    term = (keep + lax.ppermute(send, "c", SWAP)).astype(jnp.bfloat16)
    mine, _ = lax.optimization_barrier((join(gathered), send))
    other = lax.ppermute(mine, "c", SWAP)
    term = lax.all_to_all(term.reshape(-1, shard, wide), ("xh", "zh"), 0, 0)
    summed = jnp.sum(term, axis=0, dtype=jnp.float32)

    near, away = project(packed, mine, other, spot)
    away = lax.ppermute(away, CHIP, flip_y)
    near, _ = lax.optimization_barrier((near, summed))
    near = near + away
    output = near[0]
    for n, flip in enumerate(flips):
        output = output + lax.ppermute(near[n + 1], CHIP, flip)

    lines = jnp.broadcast_to(summed[None], (lax.axis_size("yh"), shard, wide))
    half = jnp.sum(lax.all_to_all(lines, "yh", 0, 0), axis=0)
    other = lax.ppermute(half, "c", SWAP)
    first = spot[0] == 0
    weight_grad = jnp.concatenate(
        [jnp.where(first, half, other), jnp.where(first, other, half)], axis=1
    )
    return output.astype(jnp.bfloat16), weight_grad


def solution(mesh):
    inner = Mesh(mesh.devices.reshape(4, 2, 2, 2, 2, 4, 2), CHIP)
    rows = P(CHIP, None)
    owners = P(("yl", "xh", "xl", "zh", "zl"), None)
    return jax.shard_map(
        local,
        mesh=inner,
        in_specs=(rows, owners, rows),
        out_specs=(rows, owners),
        check_vma=False,
    )
```

```python
import jax
import jax.numpy as jnp
from jax import lax
from jax.experimental import pallas as pl
from jax.experimental.pallas import tpu as pltpu
from jax.sharding import Mesh, PartitionSpec as P

PARAMS = pltpu.CompilerParams(vmem_limit_bytes=32 * 1024 * 1024)
ALONE = pltpu.CompilerParams(vmem_limit_bytes=60 * 1024 * 1024)
SWAP = [(0, 1), (1, 0)]
CHIP = ("yh", "c", "yl", "xh", "xl", "zh", "zl")


def pack(tokens, grad_out, shard):
    rows, width = tokens.shape
    cols = grad_out.shape[1]
    node = width // 8
    part = width // 8

    def body(t_ref, g_ref, o_ref, held, stage, t_sems, g_sems, o_sems):
        loads, sides, stores = [], [], []
        for quad in range(4):
            for xh in range(2):
                at = ((quad // 2) * 4 + xh * 2 + quad % 2) * node
                copy = pltpu.make_async_copy(
                    t_ref.at[:, pl.ds(at, node)],
                    held.at[quad * 2 + xh],
                    t_sems.at[quad * 2 + xh],
                )
                copy.start()
                loads.append(copy)
        for o in range(8):
            copy = pltpu.make_async_copy(
                g_ref, stage.at[o, :, pl.ds(part, cols)], g_sems.at[o]
            )
            copy.start()
            sides.append(copy)
        for quad in range(4):
            for xh in range(2):
                loads[quad * 2 + xh].wait()
                t = held[quad * 2 + xh]
                for zl in range(2):
                    pieces = [
                        t[:, at : at + shard]
                        for at in range(zl * shard, node, 2 * shard)
                    ]
                    stage[quad * 2 + zl, :, xh * node // 2 : (xh + 1) * node // 2] = (
                        jnp.concatenate(pieces, axis=1)
                    )
            for zl in range(2):
                o = quad * 2 + zl
                sides[o].wait()
                copy = pltpu.make_async_copy(stage.at[o], o_ref.at[o], o_sems.at[o])
                copy.start()
                stores.append(copy)
        for copy in stores:
            copy.wait()

    shape = (8, rows, part + cols)
    return pl.pallas_call(
        body,
        in_specs=[pl.BlockSpec(memory_space=pl.ANY)] * 2,
        out_specs=pl.BlockSpec(memory_space=pl.ANY),
        out_shape=jax.ShapeDtypeStruct(shape, tokens.dtype),
        scratch_shapes=[
            pltpu.VMEM((8, rows, node), tokens.dtype),
            pltpu.VMEM(shape, tokens.dtype),
        ]
        + [pltpu.SemaphoreType.DMA((8,))] * 3,
        compiler_params=ALONE,
    )(tokens, grad_out)


def terms(packed, spot, part):
    sharers, rows, both = packed.shape
    cols = both - part
    wide = cols // 2
    step = 2
    steps = sharers // step

    def body(spot_ref, p_ref, keep_ref, send_ref, stage, sems):
        loads = []
        for k in range(steps):
            at = pl.ds(k * step, step)
            loads.append(
                pltpu.make_async_copy(p_ref.at[at], stage.at[at], sems.at[k])
            )
            loads[-1].start()
        first = spot_ref[0] == 0
        for k in range(steps):
            loads[k].wait()
            p = stage[k * step : (k + 1) * step].reshape(step * rows, both)
            left, right = p[:, part : part + wide], p[:, part + wide :]
            g = jnp.concatenate(
                [jnp.where(first, left, right), jnp.where(first, right, left)], axis=1
            )
            term = lax.dot_general(
                p[:, :part],
                g,
                (((0,), (0,)), ((), ())),
                preferred_element_type=jnp.float32,
            )
            if k == 0:
                keep_ref[...] = term[:, :wide]
                send_ref[...] = term[:, wide:]
            else:
                keep_ref[...] += term[:, :wide]
                send_ref[...] += term[:, wide:]

    half = jax.ShapeDtypeStruct((part, wide), jnp.float32)
    return pl.pallas_call(
        body,
        in_specs=[
            pl.BlockSpec(memory_space=pltpu.SMEM),
            pl.BlockSpec(memory_space=pl.ANY),
        ],
        out_specs=[pl.BlockSpec(memory_space=pltpu.VMEM)] * 2,
        out_shape=[half, half],
        scratch_shapes=[
            pltpu.VMEM(packed.shape, packed.dtype),
            pltpu.SemaphoreType.DMA((steps,)),
        ],
        compiler_params=PARAMS,
    )(spot, packed)


def join(parts):
    count = len(parts)

    def body(*refs):
        o_ref, sems = refs[count:]
        copies = [
            pltpu.make_async_copy(refs[n], o_ref.at[n], sems.at[n]) for n in range(count)
        ]
        for copy in copies:
            copy.start()
        for copy in copies:
            copy.wait()

    return pl.pallas_call(
        body,
        in_specs=[pl.BlockSpec(memory_space=pl.ANY)] * count,
        out_specs=pl.BlockSpec(memory_space=pltpu.VMEM),
        out_shape=jax.ShapeDtypeStruct((count,) + parts[0].shape, parts[0].dtype),
        scratch_shapes=[pltpu.SemaphoreType.DMA((count,))],
        compiler_params=PARAMS,
    )(*parts)


def project(packed, mine, other, spot):
    sharers, rows, both = packed.shape
    depth, shard, cols = mine.shape
    part = 2 * depth * shard

    def body(spot_ref, p_ref, m_ref, r_ref, near_ref, away_ref, stage, whole, sems):
        core, yl, xl, zl, zh = (spot_ref[i] for i in range(5))
        own = (yl * 2 + xl) * 2 + zl
        loads = []
        for flip in range(sharers):
            loads.append(
                pltpu.make_async_copy(
                    p_ref.at[own ^ flip], stage.at[flip], sems.at[flip]
                )
            )
            loads[-1].start()
        for back in range(depth):
            at_z = lax.rem(zh + depth - back, depth)
            whole[core, at_z] = m_ref[back]
            whole[1 - core, at_z] = r_ref[back]
        for load in loads:
            load.wait()
        t = stage[...].reshape(sharers * rows, both)[:, :part]
        new = jnp.dot(
            t, whole[...].reshape(part, cols), preferred_element_type=jnp.float32
        ).reshape(sharers, rows, cols)
        near_ref[...] = new[: sharers // 2]
        away_ref[...] = new[sharers // 2 :]

    out = jax.ShapeDtypeStruct((sharers // 2, rows, cols), jnp.float32)
    return pl.pallas_call(
        body,
        in_specs=[
            pl.BlockSpec(memory_space=pltpu.SMEM),
            pl.BlockSpec(memory_space=pl.ANY),
        ]
        + [pl.BlockSpec(memory_space=pltpu.VMEM)] * 2,
        out_specs=[pl.BlockSpec(memory_space=pltpu.VMEM)] * 2,
        out_shape=[out, out],
        scratch_shapes=[
            pltpu.VMEM(packed.shape, packed.dtype),
            pltpu.VMEM((2, depth, shard, cols), packed.dtype),
            pltpu.SemaphoreType.DMA((sharers,)),
        ],
        compiler_params=PARAMS,
    )(spot, packed, mine, other)


def partners(sizes):
    yh, cores, yl, xh, xl, zh, zl = sizes
    rings = (yh * yl, xh * xl, zh * zl)

    def place(c, y, x, z):
        at = ((y // yl) * cores + c) * yl + y % yl
        return (at * xh * xl + x) * zh * zl + z

    def other(i, n, c):
        if c == 0:
            return i ^ 1
        return (i + 1) % n if i % 2 else (i - 1) % n

    moves = ((1, 0, 0), (0, 0, 1), (0, 1, 0), (0, 1, 1))
    flips, cubes = [[] for _ in moves], []
    for c in range(cores):
        for y in range(rings[0]):
            for x in range(rings[1]):
                for z in range(rings[2]):
                    here = (y, x, z)
                    there = [other(i, n, c) for i, n in zip(here, rings)]
                    for move, flip in zip(moves, flips):
                        to = [b if m else a for a, b, m in zip(here, there, move)]
                        flip.append((place(c, *here), place(c, *to)))
                    if all(i % 2 == 0 for i in here):
                        pairs = list(zip(here, there))
                        cubes.append(
                            [
                                place(c, a, b, d)
                                for a in pairs[0]
                                for b in pairs[1]
                                for d in pairs[2]
                            ]
                        )
    return cubes, flips[0], flips[1:]


def local(tokens, weight, grad_out):
    shard, cols = weight.shape
    wide = cols // 2
    cubes, flip_y, flips = partners([lax.axis_size(name) for name in CHIP])
    here = ("c", "yl", "xl", "zl", "zh")
    spot = jnp.stack([lax.axis_index(name) for name in here])
    spot = spot.astype(jnp.int32)

    packed = pack(tokens, grad_out, shard)
    packed = lax.all_to_all(packed, CHIP, 0, 0, axis_index_groups=cubes)
    part = packed.shape[-1] - cols
    depth = lax.axis_size("zh")
    gathered = []
    for back in range(depth):
        shift = [
            (
                (c * 2 + x) * depth + z,
                (x * 2 + (x ^ c)) * depth + (z + back) % depth,
            )
            for c in range(2)
            for x in range(2)
            for z in range(depth)
        ]
        gathered.append(lax.ppermute(weight, ("c", "xh", "zh"), shift))
    packed, *gathered = lax.optimization_barrier((packed, *gathered))

    keep, send = terms(packed, spot, part)
    term = (keep + lax.ppermute(send, "c", SWAP)).astype(jnp.bfloat16)
    mine, _ = lax.optimization_barrier((join(gathered), send))
    other = lax.ppermute(mine, "c", SWAP)
    term = lax.all_to_all(term.reshape(-1, shard, wide), ("xh", "zh"), 0, 0)
    summed = jnp.sum(term, axis=0, dtype=jnp.float32)

    near, away = project(packed, mine, other, spot)
    away = lax.ppermute(away, CHIP, flip_y)
    near, _ = lax.optimization_barrier((near, summed))
    near = near + away
    output = near[0]
    for n, flip in enumerate(flips):
        output = output + lax.ppermute(near[n + 1], CHIP, flip)

    lines = jnp.broadcast_to(summed[None], (lax.axis_size("yh"), shard, wide))
    half = jnp.sum(lax.all_to_all(lines, "yh", 0, 0), axis=0)
    other = lax.ppermute(half, "c", SWAP)
    first = spot[0] == 0
    weight_grad = jnp.concatenate(
        [jnp.where(first, half, other), jnp.where(first, other, half)], axis=1
    )
    return output.astype(jnp.bfloat16), weight_grad


def solution(mesh):
    inner = Mesh(mesh.devices.reshape(4, 2, 2, 2, 2, 4, 2), CHIP)
    rows = P(CHIP, None)
    owners = P(("yl", "xh", "xl", "zh", "zl"), None)
    return jax.shard_map(
        local,
        mesh=inner,
        in_specs=(rows, owners, rows),
        out_specs=(rows, owners),
        check_vma=False,
    )
```

```python
import jax
import jax.numpy as jnp
from jax import lax
from jax.experimental import pallas as pl
from jax.experimental.pallas import tpu as pltpu
from jax.sharding import Mesh, PartitionSpec as P

PARAMS = pltpu.CompilerParams(vmem_limit_bytes=32 * 1024 * 1024)
ALONE = pltpu.CompilerParams(vmem_limit_bytes=60 * 1024 * 1024)
SWAP = [(0, 1), (1, 0)]
CHIP = ("yh", "c", "yl", "xh", "xl", "zh", "zl")


def pack(tokens, grad_out, shard):
    rows, width = tokens.shape
    cols = grad_out.shape[1]
    node = width // 8
    part = width // 8

    def body(t_ref, g_ref, o_ref, held, stage, t_sems, g_sems, o_sems):
        loads, sides, stores = [], [], []
        for quad in range(4):
            for xh in range(2):
                at = ((quad // 2) * 4 + xh * 2 + quad % 2) * node
                copy = pltpu.make_async_copy(
                    t_ref.at[:, pl.ds(at, node)],
                    held.at[quad * 2 + xh],
                    t_sems.at[quad * 2 + xh],
                )
                copy.start()
                loads.append(copy)
        for o in range(8):
            copy = pltpu.make_async_copy(
                g_ref, stage.at[o, :, pl.ds(part, cols)], g_sems.at[o]
            )
            copy.start()
            sides.append(copy)
        for quad in range(4):
            for xh in range(2):
                loads[quad * 2 + xh].wait()
                t = held[quad * 2 + xh]
                for zl in range(2):
                    pieces = [
                        t[:, at : at + shard]
                        for at in range(zl * shard, node, 2 * shard)
                    ]
                    stage[quad * 2 + zl, :, xh * node // 2 : (xh + 1) * node // 2] = (
                        jnp.concatenate(pieces, axis=1)
                    )
            for zl in range(2):
                o = quad * 2 + zl
                sides[o].wait()
                copy = pltpu.make_async_copy(stage.at[o], o_ref.at[o], o_sems.at[o])
                copy.start()
                stores.append(copy)
        for copy in stores:
            copy.wait()

    shape = (8, rows, part + cols)
    return pl.pallas_call(
        body,
        in_specs=[pl.BlockSpec(memory_space=pl.ANY)] * 2,
        out_specs=pl.BlockSpec(memory_space=pl.ANY),
        out_shape=jax.ShapeDtypeStruct(shape, tokens.dtype),
        scratch_shapes=[
            pltpu.VMEM((8, rows, node), tokens.dtype),
            pltpu.VMEM(shape, tokens.dtype),
        ]
        + [pltpu.SemaphoreType.DMA((8,))] * 3,
        compiler_params=ALONE,
    )(tokens, grad_out)


def terms(packed, spot, part):
    sharers, rows, both = packed.shape
    cols = both - part
    wide = cols // 2
    step = 2
    steps = sharers // step

    def body(spot_ref, p_ref, keep_ref, send_ref, stage, sems):
        loads = []
        for k in range(steps):
            at = pl.ds(k * step, step)
            loads.append(
                pltpu.make_async_copy(p_ref.at[at], stage.at[at], sems.at[k])
            )
            loads[-1].start()
        first = spot_ref[0] == 0
        for k in range(steps):
            loads[k].wait()
            p = stage[k * step : (k + 1) * step].reshape(step * rows, both)
            left, right = p[:, part : part + wide], p[:, part + wide :]
            g = jnp.concatenate(
                [jnp.where(first, left, right), jnp.where(first, right, left)], axis=1
            )
            term = lax.dot_general(
                p[:, :part],
                g,
                (((0,), (0,)), ((), ())),
                preferred_element_type=jnp.float32,
            )
            if k == 0:
                keep_ref[...] = term[:, :wide]
                send_ref[...] = term[:, wide:]
            else:
                keep_ref[...] += term[:, :wide]
                send_ref[...] += term[:, wide:]

    half = jax.ShapeDtypeStruct((part, wide), jnp.float32)
    return pl.pallas_call(
        body,
        in_specs=[
            pl.BlockSpec(memory_space=pltpu.SMEM),
            pl.BlockSpec(memory_space=pl.ANY),
        ],
        out_specs=[pl.BlockSpec(memory_space=pltpu.VMEM)] * 2,
        out_shape=[half, half],
        scratch_shapes=[
            pltpu.VMEM(packed.shape, packed.dtype),
            pltpu.SemaphoreType.DMA((steps,)),
        ],
        compiler_params=PARAMS,
    )(spot, packed)


def join(parts):
    count = len(parts)

    def body(*refs):
        o_ref, sems = refs[count:]
        copies = [
            pltpu.make_async_copy(refs[n], o_ref.at[n], sems.at[n]) for n in range(count)
        ]
        for copy in copies:
            copy.start()
        for copy in copies:
            copy.wait()

    return pl.pallas_call(
        body,
        in_specs=[pl.BlockSpec(memory_space=pl.ANY)] * count,
        out_specs=pl.BlockSpec(memory_space=pltpu.VMEM),
        out_shape=jax.ShapeDtypeStruct((count,) + parts[0].shape, parts[0].dtype),
        scratch_shapes=[pltpu.SemaphoreType.DMA((count,))],
        compiler_params=PARAMS,
    )(*parts)


def project(packed, mine, other, spot):
    sharers, rows, both = packed.shape
    depth, shard, cols = mine.shape
    part = 2 * depth * shard

    def body(spot_ref, p_ref, m_ref, r_ref, near_ref, away_ref, stage, whole, sems):
        core, yl, xl, zl, zh = (spot_ref[i] for i in range(5))
        own = (yl * 2 + xl) * 2 + zl
        loads = []
        for flip in range(sharers):
            loads.append(
                pltpu.make_async_copy(
                    p_ref.at[own ^ flip], stage.at[flip], sems.at[flip]
                )
            )
            loads[-1].start()
        for back in range(depth):
            at_z = lax.rem(zh + depth - back, depth)
            whole[core, at_z] = m_ref[back]
            whole[1 - core, at_z] = r_ref[back]
        for load in loads:
            load.wait()
        t = stage[...].reshape(sharers * rows, both)[:, :part]
        new = jnp.dot(
            t, whole[...].reshape(part, cols), preferred_element_type=jnp.float32
        ).reshape(sharers, rows, cols)
        near_ref[...] = new[: sharers // 2]
        away_ref[...] = new[sharers // 2 :]

    out = jax.ShapeDtypeStruct((sharers // 2, rows, cols), jnp.float32)
    return pl.pallas_call(
        body,
        in_specs=[
            pl.BlockSpec(memory_space=pltpu.SMEM),
            pl.BlockSpec(memory_space=pl.ANY),
        ]
        + [pl.BlockSpec(memory_space=pltpu.VMEM)] * 2,
        out_specs=[pl.BlockSpec(memory_space=pltpu.VMEM)] * 2,
        out_shape=[out, out],
        scratch_shapes=[
            pltpu.VMEM(packed.shape, packed.dtype),
            pltpu.VMEM((2, depth, shard, cols), packed.dtype),
            pltpu.SemaphoreType.DMA((sharers,)),
        ],
        compiler_params=PARAMS,
    )(spot, packed, mine, other)


def partners(sizes):
    yh, cores, yl, xh, xl, zh, zl = sizes
    rings = (yh * yl, xh * xl, zh * zl)

    def place(c, y, x, z):
        at = ((y // yl) * cores + c) * yl + y % yl
        return (at * xh * xl + x) * zh * zl + z

    def other(i, n, c):
        if c == 0:
            return i ^ 1
        return (i + 1) % n if i % 2 else (i - 1) % n

    moves = ((1, 0, 0), (0, 1, 0), (0, 0, 1))
    flips, cubes = [[] for _ in moves], []
    for c in range(cores):
        for y in range(rings[0]):
            for x in range(rings[1]):
                for z in range(rings[2]):
                    here = (y, x, z)
                    there = [other(i, n, c) for i, n in zip(here, rings)]
                    for move, flip in zip(moves, flips):
                        to = [b if m else a for a, b, m in zip(here, there, move)]
                        flip.append((place(c, *here), place(c, *to)))
                    if all(i % 2 == 0 for i in here):
                        pairs = list(zip(here, there))
                        cubes.append(
                            [
                                place(c, a, b, d)
                                for a in pairs[0]
                                for b in pairs[1]
                                for d in pairs[2]
                            ]
                        )
    return cubes, *flips


def local(tokens, weight, grad_out):
    shard, cols = weight.shape
    wide = cols // 2
    cubes, flip_y, flip_x, flip_z = partners([lax.axis_size(name) for name in CHIP])
    here = ("c", "yl", "xl", "zl", "zh")
    spot = jnp.stack([lax.axis_index(name) for name in here])
    spot = spot.astype(jnp.int32)

    packed = pack(tokens, grad_out, shard)
    packed = lax.all_to_all(packed, CHIP, 0, 0, axis_index_groups=cubes)
    part = packed.shape[-1] - cols
    depth = lax.axis_size("zh")
    gathered = []
    for back in range(depth):
        shift = [
            (
                (c * 2 + x) * depth + z,
                (x * 2 + (x ^ c)) * depth + (z + back) % depth,
            )
            for c in range(2)
            for x in range(2)
            for z in range(depth)
        ]
        gathered.append(lax.ppermute(weight, ("c", "xh", "zh"), shift))
    packed, *gathered = lax.optimization_barrier((packed, *gathered))

    keep, send = terms(packed, spot, part)
    term = (keep + lax.ppermute(send, "c", SWAP)).astype(jnp.bfloat16)
    mine, _ = lax.optimization_barrier((join(gathered), send))
    other = lax.ppermute(mine, "c", SWAP)
    term = lax.all_to_all(term.reshape(-1, shard, wide), ("xh", "zh"), 0, 0)
    summed = jnp.sum(term, axis=0, dtype=jnp.float32)

    near, away = project(packed, mine, other, spot)
    away = lax.ppermute(away, CHIP, flip_y)
    near, _ = lax.optimization_barrier((near, summed))
    near = near + away
    near = near[:2] + lax.ppermute(near[2:], CHIP, flip_x)

    lines = jnp.broadcast_to(summed[None], (lax.axis_size("yh"), shard, wide))
    lines = lax.all_to_all(lines, "yh", 0, 0)
    near, lines = lax.optimization_barrier((near, lines))
    half = jnp.sum(lines, axis=0)
    other = lax.ppermute(half, "c", SWAP)
    output = near[0] + lax.ppermute(near[1], CHIP, flip_z)
    first = spot[0] == 0
    weight_grad = jnp.concatenate(
        [jnp.where(first, half, other), jnp.where(first, other, half)], axis=1
    )
    return output.astype(jnp.bfloat16), weight_grad


def solution(mesh):
    inner = Mesh(mesh.devices.reshape(4, 2, 2, 2, 2, 4, 2), CHIP)
    rows = P(CHIP, None)
    owners = P(("yl", "xh", "xl", "zh", "zl"), None)
    return jax.shard_map(
        local,
        mesh=inner,
        in_specs=(rows, owners, rows),
        out_specs=(rows, owners),
        check_vma=False,
    )
```

```python
import jax
import jax.numpy as jnp
from jax import lax
from jax.experimental import pallas as pl
from jax.experimental.pallas import tpu as pltpu
from jax.sharding import Mesh, PartitionSpec as P

PARAMS = pltpu.CompilerParams(vmem_limit_bytes=32 * 1024 * 1024)
ALONE = pltpu.CompilerParams(vmem_limit_bytes=60 * 1024 * 1024)
SWAP = [(0, 1), (1, 0)]
CHIP = ("yh", "c", "yl", "xh", "xl", "zh", "zl")


def pack(tokens, grad_out, shard):
    rows, width = tokens.shape
    cols = grad_out.shape[1]
    node = width // 8
    part = width // 8

    def body(t_ref, g_ref, o_ref, held, stage, t_sems, g_sems, o_sems):
        loads, sides, stores = [], [], []
        for quad in range(4):
            for xh in range(2):
                at = ((quad // 2) * 4 + xh * 2 + quad % 2) * node
                copy = pltpu.make_async_copy(
                    t_ref.at[:, pl.ds(at, node)],
                    held.at[quad * 2 + xh],
                    t_sems.at[quad * 2 + xh],
                )
                copy.start()
                loads.append(copy)
        for o in range(8):
            copy = pltpu.make_async_copy(
                g_ref, stage.at[o, :, pl.ds(part, cols)], g_sems.at[o]
            )
            copy.start()
            sides.append(copy)
        for quad in range(4):
            for xh in range(2):
                loads[quad * 2 + xh].wait()
                t = held[quad * 2 + xh]
                for zl in range(2):
                    pieces = [
                        t[:, at : at + shard]
                        for at in range(zl * shard, node, 2 * shard)
                    ]
                    stage[quad * 2 + zl, :, xh * node // 2 : (xh + 1) * node // 2] = (
                        jnp.concatenate(pieces, axis=1)
                    )
            for zl in range(2):
                o = quad * 2 + zl
                sides[o].wait()
                copy = pltpu.make_async_copy(stage.at[o], o_ref.at[o], o_sems.at[o])
                copy.start()
                stores.append(copy)
        for copy in stores:
            copy.wait()

    shape = (8, rows, part + cols)
    return pl.pallas_call(
        body,
        in_specs=[pl.BlockSpec(memory_space=pl.ANY)] * 2,
        out_specs=pl.BlockSpec(memory_space=pl.ANY),
        out_shape=jax.ShapeDtypeStruct(shape, tokens.dtype),
        scratch_shapes=[
            pltpu.VMEM((8, rows, node), tokens.dtype),
            pltpu.VMEM(shape, tokens.dtype),
        ]
        + [pltpu.SemaphoreType.DMA((8,))] * 3,
        compiler_params=ALONE,
    )(tokens, grad_out)


def terms(packed, spot, part):
    sharers, rows, both = packed.shape
    cols = both - part
    wide = cols // 2
    step = 2
    steps = sharers // step

    def body(spot_ref, p_ref, keep_ref, send_ref, stage, sems):
        loads = []
        for k in range(steps):
            at = pl.ds(k * step, step)
            loads.append(
                pltpu.make_async_copy(p_ref.at[at], stage.at[at], sems.at[k])
            )
            loads[-1].start()
        first = spot_ref[0] == 0
        for k in range(steps):
            loads[k].wait()
            p = stage[k * step : (k + 1) * step].reshape(step * rows, both)
            left, right = p[:, part : part + wide], p[:, part + wide :]
            g = jnp.concatenate(
                [jnp.where(first, left, right), jnp.where(first, right, left)], axis=1
            )
            term = lax.dot_general(
                p[:, :part],
                g,
                (((0,), (0,)), ((), ())),
                preferred_element_type=jnp.float32,
            )
            if k == 0:
                keep_ref[...] = term[:, :wide]
                send_ref[...] = term[:, wide:]
            else:
                keep_ref[...] += term[:, :wide]
                send_ref[...] += term[:, wide:]

    half = jax.ShapeDtypeStruct((part, wide), jnp.float32)
    return pl.pallas_call(
        body,
        in_specs=[
            pl.BlockSpec(memory_space=pltpu.SMEM),
            pl.BlockSpec(memory_space=pl.ANY),
        ],
        out_specs=[pl.BlockSpec(memory_space=pltpu.VMEM)] * 2,
        out_shape=[half, half],
        scratch_shapes=[
            pltpu.VMEM(packed.shape, packed.dtype),
            pltpu.SemaphoreType.DMA((steps,)),
        ],
        compiler_params=PARAMS,
    )(spot, packed)


def join(parts):
    count = len(parts)

    def body(*refs):
        o_ref, sems = refs[count:]
        copies = [
            pltpu.make_async_copy(refs[n], o_ref.at[n], sems.at[n]) for n in range(count)
        ]
        for copy in copies:
            copy.start()
        for copy in copies:
            copy.wait()

    return pl.pallas_call(
        body,
        in_specs=[pl.BlockSpec(memory_space=pl.ANY)] * count,
        out_specs=pl.BlockSpec(memory_space=pltpu.VMEM),
        out_shape=jax.ShapeDtypeStruct((count,) + parts[0].shape, parts[0].dtype),
        scratch_shapes=[pltpu.SemaphoreType.DMA((count,))],
        compiler_params=PARAMS,
    )(*parts)


def project(packed, mine, other, spot):
    sharers, rows, both = packed.shape
    depth, shard, cols = mine.shape
    part = 2 * depth * shard

    def body(spot_ref, p_ref, m_ref, r_ref, near_ref, away_ref, stage, whole, sems):
        core, yl, xl, zl, zh = (spot_ref[i] for i in range(5))
        own = (yl * 2 + xl) * 2 + zl
        loads = []
        for n, flip in enumerate((0, 1, 4, 5, 2, 3, 6, 7)):
            loads.append(
                pltpu.make_async_copy(p_ref.at[own ^ flip], stage.at[n], sems.at[n])
            )
            loads[-1].start()
        for back in range(depth):
            at_z = lax.rem(zh + depth - back, depth)
            whole[core, at_z] = m_ref[back]
            whole[1 - core, at_z] = r_ref[back]
        for load in loads:
            load.wait()
        t = stage[...].reshape(sharers * rows, both)[:, :part]
        new = jnp.dot(
            t, whole[...].reshape(part, cols), preferred_element_type=jnp.float32
        ).reshape(sharers, rows, cols)
        near_ref[...] = new[: sharers // 2]
        away_ref[...] = new[sharers // 2 :]

    out = jax.ShapeDtypeStruct((sharers // 2, rows, cols), jnp.float32)
    return pl.pallas_call(
        body,
        in_specs=[
            pl.BlockSpec(memory_space=pltpu.SMEM),
            pl.BlockSpec(memory_space=pl.ANY),
        ]
        + [pl.BlockSpec(memory_space=pltpu.VMEM)] * 2,
        out_specs=[pl.BlockSpec(memory_space=pltpu.VMEM)] * 2,
        out_shape=[out, out],
        scratch_shapes=[
            pltpu.VMEM(packed.shape, packed.dtype),
            pltpu.VMEM((2, depth, shard, cols), packed.dtype),
            pltpu.SemaphoreType.DMA((sharers,)),
        ],
        compiler_params=PARAMS,
    )(spot, packed, mine, other)


def partners(sizes):
    yh, cores, yl, xh, xl, zh, zl = sizes
    rings = (yh * yl, xh * xl, zh * zl)

    def place(c, y, x, z):
        at = ((y // yl) * cores + c) * yl + y % yl
        return (at * xh * xl + x) * zh * zl + z

    def other(i, n, c):
        if c == 0:
            return i ^ 1
        return (i + 1) % n if i % 2 else (i - 1) % n

    moves = ((0, 1, 0), (0, 0, 1), (1, 0, 0), (1, 0, 1))
    flips, cubes = [[] for _ in moves], []
    for c in range(cores):
        for y in range(rings[0]):
            for x in range(rings[1]):
                for z in range(rings[2]):
                    here = (y, x, z)
                    there = [other(i, n, c) for i, n in zip(here, rings)]
                    for move, flip in zip(moves, flips):
                        to = [b if m else a for a, b, m in zip(here, there, move)]
                        flip.append((place(c, *here), place(c, *to)))
                    if all(i % 2 == 0 for i in here):
                        pairs = list(zip(here, there))
                        cubes.append(
                            [
                                place(c, a, b, d)
                                for a in pairs[0]
                                for b in pairs[1]
                                for d in pairs[2]
                            ]
                        )
    return cubes, flips[0], flips[1:]


def local(tokens, weight, grad_out):
    shard, cols = weight.shape
    wide = cols // 2
    cubes, flip_x, flips = partners([lax.axis_size(name) for name in CHIP])
    here = ("c", "yl", "xl", "zl", "zh")
    spot = jnp.stack([lax.axis_index(name) for name in here])
    spot = spot.astype(jnp.int32)

    packed = pack(tokens, grad_out, shard)
    packed = lax.all_to_all(packed, CHIP, 0, 0, axis_index_groups=cubes)
    part = packed.shape[-1] - cols
    depth = lax.axis_size("zh")
    gathered = []
    for back in range(depth):
        shift = [
            (
                (c * 2 + x) * depth + z,
                (x * 2 + (x ^ c)) * depth + (z + back) % depth,
            )
            for c in range(2)
            for x in range(2)
            for z in range(depth)
        ]
        gathered.append(lax.ppermute(weight, ("c", "xh", "zh"), shift))
    packed, *gathered = lax.optimization_barrier((packed, *gathered))

    keep, send = terms(packed, spot, part)
    term = (keep + lax.ppermute(send, "c", SWAP)).astype(jnp.bfloat16)
    mine, _ = lax.optimization_barrier((join(gathered), send))
    other = lax.ppermute(mine, "c", SWAP)
    term = lax.all_to_all(term.reshape(-1, shard, wide), ("xh", "zh"), 0, 0)
    summed = jnp.sum(term, axis=0, dtype=jnp.float32)

    near, away = project(packed, mine, other, spot)
    away = lax.ppermute(away, CHIP, flip_x)
    near, _ = lax.optimization_barrier((near, summed))
    near = near + away
    output = near[0]
    for n, flip in enumerate(flips):
        output = output + lax.ppermute(near[n + 1], CHIP, flip)

    lines = jnp.broadcast_to(summed[None], (lax.axis_size("yh"), shard, wide))
    half = jnp.sum(lax.all_to_all(lines, "yh", 0, 0), axis=0)
    other = lax.ppermute(half, "c", SWAP)
    first = spot[0] == 0
    weight_grad = jnp.concatenate(
        [jnp.where(first, half, other), jnp.where(first, other, half)], axis=1
    )
    return output.astype(jnp.bfloat16), weight_grad


def solution(mesh):
    inner = Mesh(mesh.devices.reshape(4, 2, 2, 2, 2, 4, 2), CHIP)
    rows = P(CHIP, None)
    owners = P(("yl", "xh", "xl", "zh", "zl"), None)
    return jax.shard_map(
        local,
        mesh=inner,
        in_specs=(rows, owners, rows),
        out_specs=(rows, owners),
        check_vma=False,
    )
```

```python
import jax
import jax.numpy as jnp
from jax import lax
from jax.experimental import pallas as pl
from jax.experimental.pallas import tpu as pltpu
from jax.sharding import Mesh, PartitionSpec as P

PARAMS = pltpu.CompilerParams(vmem_limit_bytes=32 * 1024 * 1024)
ALONE = pltpu.CompilerParams(vmem_limit_bytes=60 * 1024 * 1024)
SWAP = [(0, 1), (1, 0)]
CHIP = ("yh", "c", "yl", "xh", "xl", "zh", "zl")


def pack(tokens, grad_out, shard):
    rows, width = tokens.shape
    cols = grad_out.shape[1]
    node = width // 8
    part = width // 8

    def body(t_ref, g_ref, o_ref, held, stage, t_sems, g_sems, o_sems):
        loads, sides, stores = [], [], []
        for quad in range(4):
            for xh in range(2):
                at = ((quad // 2) * 4 + xh * 2 + quad % 2) * node
                copy = pltpu.make_async_copy(
                    t_ref.at[:, pl.ds(at, node)],
                    held.at[quad * 2 + xh],
                    t_sems.at[quad * 2 + xh],
                )
                copy.start()
                loads.append(copy)
        for o in range(8):
            copy = pltpu.make_async_copy(
                g_ref, stage.at[o, :, pl.ds(part, cols)], g_sems.at[o]
            )
            copy.start()
            sides.append(copy)
        for quad in range(4):
            for xh in range(2):
                loads[quad * 2 + xh].wait()
                t = held[quad * 2 + xh]
                for zl in range(2):
                    pieces = [
                        t[:, at : at + shard]
                        for at in range(zl * shard, node, 2 * shard)
                    ]
                    stage[quad * 2 + zl, :, xh * node // 2 : (xh + 1) * node // 2] = (
                        jnp.concatenate(pieces, axis=1)
                    )
            for zl in range(2):
                o = quad * 2 + zl
                sides[o].wait()
                copy = pltpu.make_async_copy(stage.at[o], o_ref.at[o], o_sems.at[o])
                copy.start()
                stores.append(copy)
        for copy in stores:
            copy.wait()

    shape = (8, rows, part + cols)
    return pl.pallas_call(
        body,
        in_specs=[pl.BlockSpec(memory_space=pl.ANY)] * 2,
        out_specs=pl.BlockSpec(memory_space=pl.ANY),
        out_shape=jax.ShapeDtypeStruct(shape, tokens.dtype),
        scratch_shapes=[
            pltpu.VMEM((8, rows, node), tokens.dtype),
            pltpu.VMEM(shape, tokens.dtype),
        ]
        + [pltpu.SemaphoreType.DMA((8,))] * 3,
        compiler_params=ALONE,
    )(tokens, grad_out)


def terms(packed, spot, part):
    sharers, rows, both = packed.shape
    cols = both - part
    wide = cols // 2
    step = 2
    steps = sharers // step

    def body(spot_ref, p_ref, keep_ref, send_ref, stage, sems):
        loads = []
        for k in range(steps):
            at = pl.ds(k * step, step)
            loads.append(
                pltpu.make_async_copy(p_ref.at[at], stage.at[at], sems.at[k])
            )
            loads[-1].start()
        first = spot_ref[0] == 0
        for k in range(steps):
            loads[k].wait()
            p = stage[k * step : (k + 1) * step].reshape(step * rows, both)
            left, right = p[:, part : part + wide], p[:, part + wide :]
            g = jnp.concatenate(
                [jnp.where(first, left, right), jnp.where(first, right, left)], axis=1
            )
            term = lax.dot_general(
                p[:, :part],
                g,
                (((0,), (0,)), ((), ())),
                preferred_element_type=jnp.float32,
            )
            if k == 0:
                keep_ref[...] = term[:, :wide]
                send_ref[...] = term[:, wide:]
            else:
                keep_ref[...] += term[:, :wide]
                send_ref[...] += term[:, wide:]

    half = jax.ShapeDtypeStruct((part, wide), jnp.float32)
    return pl.pallas_call(
        body,
        in_specs=[
            pl.BlockSpec(memory_space=pltpu.SMEM),
            pl.BlockSpec(memory_space=pl.ANY),
        ],
        out_specs=[pl.BlockSpec(memory_space=pltpu.VMEM)] * 2,
        out_shape=[half, half],
        scratch_shapes=[
            pltpu.VMEM(packed.shape, packed.dtype),
            pltpu.SemaphoreType.DMA((steps,)),
        ],
        compiler_params=PARAMS,
    )(spot, packed)


def join(parts):
    count = len(parts)

    def body(*refs):
        o_ref, sems = refs[count:]
        copies = [
            pltpu.make_async_copy(refs[n], o_ref.at[n], sems.at[n]) for n in range(count)
        ]
        for copy in copies:
            copy.start()
        for copy in copies:
            copy.wait()

    return pl.pallas_call(
        body,
        in_specs=[pl.BlockSpec(memory_space=pl.ANY)] * count,
        out_specs=pl.BlockSpec(memory_space=pltpu.VMEM),
        out_shape=jax.ShapeDtypeStruct((count,) + parts[0].shape, parts[0].dtype),
        scratch_shapes=[pltpu.SemaphoreType.DMA((count,))],
        compiler_params=PARAMS,
    )(*parts)


def project(packed, mine, other, spot):
    sharers, rows, both = packed.shape
    depth, shard, cols = mine.shape
    part = 2 * depth * shard

    def body(spot_ref, p_ref, m_ref, r_ref, near_ref, away_ref, stage, whole, sems):
        core, yl, xl, zl, zh = (spot_ref[i] for i in range(5))
        own = (yl * 2 + xl) * 2 + zl
        loads = []
        for n, flip in enumerate((0, 1, 4, 5, 2, 3, 6, 7)):
            loads.append(
                pltpu.make_async_copy(p_ref.at[own ^ flip], stage.at[n], sems.at[n])
            )
            loads[-1].start()
        for back in range(depth):
            at_z = lax.rem(zh + depth - back, depth)
            whole[core, at_z] = m_ref[back]
            whole[1 - core, at_z] = r_ref[back]
        for load in loads:
            load.wait()
        t = stage[...].reshape(sharers * rows, both)[:, :part]
        new = jnp.dot(
            t, whole[...].reshape(part, cols), preferred_element_type=jnp.float32
        ).reshape(sharers, rows, cols)
        near_ref[...] = new[: sharers // 2]
        away_ref[...] = new[sharers // 2 :]

    out = jax.ShapeDtypeStruct((sharers // 2, rows, cols), jnp.float32)
    return pl.pallas_call(
        body,
        in_specs=[
            pl.BlockSpec(memory_space=pltpu.SMEM),
            pl.BlockSpec(memory_space=pl.ANY),
        ]
        + [pl.BlockSpec(memory_space=pltpu.VMEM)] * 2,
        out_specs=[pl.BlockSpec(memory_space=pltpu.VMEM)] * 2,
        out_shape=[out, out],
        scratch_shapes=[
            pltpu.VMEM(packed.shape, packed.dtype),
            pltpu.VMEM((2, depth, shard, cols), packed.dtype),
            pltpu.SemaphoreType.DMA((sharers,)),
        ],
        compiler_params=PARAMS,
    )(spot, packed, mine, other)


def partners(sizes):
    yh, cores, yl, xh, xl, zh, zl = sizes
    rings = (yh * yl, xh * xl, zh * zl)

    def place(c, y, x, z):
        at = ((y // yl) * cores + c) * yl + y % yl
        return (at * xh * xl + x) * zh * zl + z

    def other(i, n, c):
        if c == 0:
            return i ^ 1
        return (i + 1) % n if i % 2 else (i - 1) % n

    moves = ((0, 1, 0), (0, 0, 1), (1, 0, 0), (1, 0, 1))
    flips, cubes = [[] for _ in moves], []
    for c in range(cores):
        for y in range(rings[0]):
            for x in range(rings[1]):
                for z in range(rings[2]):
                    here = (y, x, z)
                    there = [other(i, n, c) for i, n in zip(here, rings)]
                    for move, flip in zip(moves, flips):
                        to = [b if m else a for a, b, m in zip(here, there, move)]
                        flip.append((place(c, *here), place(c, *to)))
                    if all(i % 2 == 0 for i in here):
                        pairs = list(zip(here, there))
                        cubes.append(
                            [
                                place(c, a, b, d)
                                for a in pairs[0]
                                for b in pairs[1]
                                for d in pairs[2]
                            ]
                        )
    return cubes, flips[0], flips[1:]


def local(tokens, weight, grad_out):
    shard, cols = weight.shape
    wide = cols // 2
    cubes, flip_x, flips = partners([lax.axis_size(name) for name in CHIP])
    here = ("c", "yl", "xl", "zl", "zh")
    spot = jnp.stack([lax.axis_index(name) for name in here])
    spot = spot.astype(jnp.int32)

    packed = pack(tokens, grad_out, shard)
    packed = lax.all_to_all(packed, CHIP, 0, 0, axis_index_groups=cubes)
    part = packed.shape[-1] - cols
    depth = lax.axis_size("zh")
    gathered = []
    for back in range(depth):
        shift = [
            (
                (c * 2 + x) * depth + z,
                (x * 2 + (x ^ c)) * depth + (z + back) % depth,
            )
            for c in range(2)
            for x in range(2)
            for z in range(depth)
        ]
        gathered.append(lax.ppermute(weight, ("c", "xh", "zh"), shift))
    packed, *gathered = lax.optimization_barrier((packed, *gathered))

    keep, send = terms(packed, spot, part)
    term = (keep + lax.ppermute(send, "c", SWAP)).astype(jnp.bfloat16)
    mine, _ = lax.optimization_barrier((join(gathered), send))
    other = lax.ppermute(mine, "c", SWAP)
    term, other = lax.optimization_barrier((term, other))
    term = lax.all_to_all(term.reshape(-1, shard, wide), ("xh", "zh"), 0, 0)
    summed = jnp.sum(term, axis=0, dtype=jnp.float32)

    near, away = project(packed, mine, other, spot)
    away = lax.ppermute(away, CHIP, flip_x)
    near, _ = lax.optimization_barrier((near, summed))
    near = near + away
    output = near[0]
    for n, flip in enumerate(flips):
        output = output + lax.ppermute(near[n + 1], CHIP, flip)

    lines = jnp.broadcast_to(summed[None], (lax.axis_size("yh"), shard, wide))
    half = jnp.sum(lax.all_to_all(lines, "yh", 0, 0), axis=0)
    other = lax.ppermute(half, "c", SWAP)
    first = spot[0] == 0
    weight_grad = jnp.concatenate(
        [jnp.where(first, half, other), jnp.where(first, other, half)], axis=1
    )
    return output.astype(jnp.bfloat16), weight_grad


def solution(mesh):
    inner = Mesh(mesh.devices.reshape(4, 2, 2, 2, 2, 4, 2), CHIP)
    rows = P(CHIP, None)
    owners = P(("yl", "xh", "xl", "zh", "zl"), None)
    return jax.shard_map(
        local,
        mesh=inner,
        in_specs=(rows, owners, rows),
        out_specs=(rows, owners),
        check_vma=False,
    )
```

```python
import jax
import jax.numpy as jnp
from jax import lax
from jax.experimental import pallas as pl
from jax.experimental.pallas import tpu as pltpu
from jax.sharding import Mesh, PartitionSpec as P

PARAMS = pltpu.CompilerParams(vmem_limit_bytes=32 * 1024 * 1024)
ALONE = pltpu.CompilerParams(vmem_limit_bytes=60 * 1024 * 1024)
SWAP = [(0, 1), (1, 0)]
CHIP = ("yh", "c", "yl", "xh", "xl", "zh", "zl")


def pack(tokens, grad_out, shard):
    rows, width = tokens.shape
    cols = grad_out.shape[1]
    node = width // 8
    part = width // 8

    def body(t_ref, g_ref, o_ref, held, stage, t_sems, g_sems, o_sems):
        loads, sides, stores = [], [], []
        for quad in range(4):
            for xh in range(2):
                at = ((quad // 2) * 4 + xh * 2 + quad % 2) * node
                copy = pltpu.make_async_copy(
                    t_ref.at[:, pl.ds(at, node)],
                    held.at[quad * 2 + xh],
                    t_sems.at[quad * 2 + xh],
                )
                copy.start()
                loads.append(copy)
        for o in range(8):
            copy = pltpu.make_async_copy(
                g_ref, stage.at[o, :, pl.ds(part, cols)], g_sems.at[o]
            )
            copy.start()
            sides.append(copy)
        for quad in range(4):
            for xh in range(2):
                loads[quad * 2 + xh].wait()
                t = held[quad * 2 + xh]
                for zl in range(2):
                    pieces = [
                        t[:, at : at + shard]
                        for at in range(zl * shard, node, 2 * shard)
                    ]
                    stage[quad * 2 + zl, :, xh * node // 2 : (xh + 1) * node // 2] = (
                        jnp.concatenate(pieces, axis=1)
                    )
            for zl in range(2):
                o = quad * 2 + zl
                sides[o].wait()
                copy = pltpu.make_async_copy(stage.at[o], o_ref.at[o], o_sems.at[o])
                copy.start()
                stores.append(copy)
        for copy in stores:
            copy.wait()

    shape = (8, rows, part + cols)
    return pl.pallas_call(
        body,
        in_specs=[pl.BlockSpec(memory_space=pl.ANY)] * 2,
        out_specs=pl.BlockSpec(memory_space=pl.ANY),
        out_shape=jax.ShapeDtypeStruct(shape, tokens.dtype),
        scratch_shapes=[
            pltpu.VMEM((8, rows, node), tokens.dtype),
            pltpu.VMEM(shape, tokens.dtype),
        ]
        + [pltpu.SemaphoreType.DMA((8,))] * 3,
        compiler_params=ALONE,
    )(tokens, grad_out)


def terms(packed, spot, part):
    sharers, rows, both = packed.shape
    cols = both - part
    wide = cols // 2
    step = 4
    steps = sharers // step

    def body(spot_ref, p_ref, keep_ref, send_ref, stage, sems):
        loads = []
        for k in range(steps):
            at = pl.ds(k * step, step)
            loads.append(
                pltpu.make_async_copy(p_ref.at[at], stage.at[at], sems.at[k])
            )
            loads[-1].start()
        first = spot_ref[0] == 0
        for k in range(steps):
            loads[k].wait()
            p = stage[k * step : (k + 1) * step].reshape(step * rows, both)
            left, right = p[:, part : part + wide], p[:, part + wide :]
            g = jnp.concatenate(
                [jnp.where(first, left, right), jnp.where(first, right, left)], axis=1
            )
            term = lax.dot_general(
                p[:, :part],
                g,
                (((0,), (0,)), ((), ())),
                preferred_element_type=jnp.float32,
            )
            if k == 0:
                keep_ref[...] = term[:, :wide]
                send_ref[...] = term[:, wide:]
            else:
                keep_ref[...] += term[:, :wide]
                send_ref[...] += term[:, wide:]

    half = jax.ShapeDtypeStruct((part, wide), jnp.float32)
    return pl.pallas_call(
        body,
        in_specs=[
            pl.BlockSpec(memory_space=pltpu.SMEM),
            pl.BlockSpec(memory_space=pl.ANY),
        ],
        out_specs=[pl.BlockSpec(memory_space=pltpu.VMEM)] * 2,
        out_shape=[half, half],
        scratch_shapes=[
            pltpu.VMEM(packed.shape, packed.dtype),
            pltpu.SemaphoreType.DMA((steps,)),
        ],
        compiler_params=PARAMS,
    )(spot, packed)


def join(parts):
    count = len(parts)

    def body(*refs):
        o_ref, sems = refs[count:]
        copies = [
            pltpu.make_async_copy(refs[n], o_ref.at[n], sems.at[n]) for n in range(count)
        ]
        for copy in copies:
            copy.start()
        for copy in copies:
            copy.wait()

    return pl.pallas_call(
        body,
        in_specs=[pl.BlockSpec(memory_space=pl.ANY)] * count,
        out_specs=pl.BlockSpec(memory_space=pltpu.VMEM),
        out_shape=jax.ShapeDtypeStruct((count,) + parts[0].shape, parts[0].dtype),
        scratch_shapes=[pltpu.SemaphoreType.DMA((count,))],
        compiler_params=PARAMS,
    )(*parts)


def project(packed, mine, other, spot):
    sharers, rows, both = packed.shape
    depth, shard, cols = mine.shape
    part = 2 * depth * shard

    def body(spot_ref, p_ref, m_ref, r_ref, near_ref, away_ref, stage, whole, sems):
        core, yl, xl, zl, zh = (spot_ref[i] for i in range(5))
        own = (yl * 2 + xl) * 2 + zl
        loads = []
        for n, flip in enumerate((0, 1, 4, 5, 2, 3, 6, 7)):
            loads.append(
                pltpu.make_async_copy(p_ref.at[own ^ flip], stage.at[n], sems.at[n])
            )
            loads[-1].start()
        for back in range(depth):
            at_z = lax.rem(zh + depth - back, depth)
            whole[core, at_z] = m_ref[back]
            whole[1 - core, at_z] = r_ref[back]
        for load in loads:
            load.wait()
        t = stage[...].reshape(sharers * rows, both)[:, :part]
        new = jnp.dot(
            t, whole[...].reshape(part, cols), preferred_element_type=jnp.float32
        ).reshape(sharers, rows, cols)
        near_ref[...] = new[: sharers // 2]
        away_ref[...] = new[sharers // 2 :]

    out = jax.ShapeDtypeStruct((sharers // 2, rows, cols), jnp.float32)
    return pl.pallas_call(
        body,
        in_specs=[
            pl.BlockSpec(memory_space=pltpu.SMEM),
            pl.BlockSpec(memory_space=pl.ANY),
        ]
        + [pl.BlockSpec(memory_space=pltpu.VMEM)] * 2,
        out_specs=[pl.BlockSpec(memory_space=pltpu.VMEM)] * 2,
        out_shape=[out, out],
        scratch_shapes=[
            pltpu.VMEM(packed.shape, packed.dtype),
            pltpu.VMEM((2, depth, shard, cols), packed.dtype),
            pltpu.SemaphoreType.DMA((sharers,)),
        ],
        compiler_params=PARAMS,
    )(spot, packed, mine, other)


def partners(sizes):
    yh, cores, yl, xh, xl, zh, zl = sizes
    rings = (yh * yl, xh * xl, zh * zl)

    def place(c, y, x, z):
        at = ((y // yl) * cores + c) * yl + y % yl
        return (at * xh * xl + x) * zh * zl + z

    def other(i, n, c):
        if c == 0:
            return i ^ 1
        return (i + 1) % n if i % 2 else (i - 1) % n

    moves = ((0, 1, 0), (0, 0, 1), (1, 0, 0), (1, 0, 1))
    flips, cubes = [[] for _ in moves], []
    for c in range(cores):
        for y in range(rings[0]):
            for x in range(rings[1]):
                for z in range(rings[2]):
                    here = (y, x, z)
                    there = [other(i, n, c) for i, n in zip(here, rings)]
                    for move, flip in zip(moves, flips):
                        to = [b if m else a for a, b, m in zip(here, there, move)]
                        flip.append((place(c, *here), place(c, *to)))
                    if all(i % 2 == 0 for i in here):
                        pairs = list(zip(here, there))
                        cubes.append(
                            [
                                place(c, a, b, d)
                                for a in pairs[0]
                                for b in pairs[1]
                                for d in pairs[2]
                            ]
                        )
    return cubes, flips[0], flips[1:]


def local(tokens, weight, grad_out):
    shard, cols = weight.shape
    wide = cols // 2
    cubes, flip_x, flips = partners([lax.axis_size(name) for name in CHIP])
    here = ("c", "yl", "xl", "zl", "zh")
    spot = jnp.stack([lax.axis_index(name) for name in here])
    spot = spot.astype(jnp.int32)

    packed = pack(tokens, grad_out, shard)
    packed = lax.all_to_all(packed, CHIP, 0, 0, axis_index_groups=cubes)
    part = packed.shape[-1] - cols
    depth = lax.axis_size("zh")
    gathered = []
    for back in range(depth):
        shift = [
            (
                (c * 2 + x) * depth + z,
                (x * 2 + (x ^ c)) * depth + (z + back) % depth,
            )
            for c in range(2)
            for x in range(2)
            for z in range(depth)
        ]
        gathered.append(lax.ppermute(weight, ("c", "xh", "zh"), shift))
    packed, *gathered = lax.optimization_barrier((packed, *gathered))

    keep, send = terms(packed, spot, part)
    term = (keep + lax.ppermute(send, "c", SWAP)).astype(jnp.bfloat16)
    mine, _ = lax.optimization_barrier((join(gathered), send))
    other = lax.ppermute(mine, "c", SWAP)
    term = lax.all_to_all(term.reshape(-1, shard, wide), ("xh", "zh"), 0, 0)
    summed = jnp.sum(term, axis=0, dtype=jnp.float32)

    near, away = project(packed, mine, other, spot)
    away = lax.ppermute(away, CHIP, flip_x)
    near, _ = lax.optimization_barrier((near, summed))
    near = near + away
    output = near[0]
    for n, flip in enumerate(flips):
        output = output + lax.ppermute(near[n + 1], CHIP, flip)

    lines = jnp.broadcast_to(summed[None], (lax.axis_size("yh"), shard, wide))
    half = jnp.sum(lax.all_to_all(lines, "yh", 0, 0), axis=0)
    other = lax.ppermute(half, "c", SWAP)
    first = spot[0] == 0
    weight_grad = jnp.concatenate(
        [jnp.where(first, half, other), jnp.where(first, other, half)], axis=1
    )
    return output.astype(jnp.bfloat16), weight_grad


def solution(mesh):
    inner = Mesh(mesh.devices.reshape(4, 2, 2, 2, 2, 4, 2), CHIP)
    rows = P(CHIP, None)
    owners = P(("yl", "xh", "xl", "zh", "zl"), None)
    return jax.shard_map(
        local,
        mesh=inner,
        in_specs=(rows, owners, rows),
        out_specs=(rows, owners),
        check_vma=False,
    )
```
